128 devices in a mesh: dp: 4 (over z), mp: 32 (over x, y, core).
Axes of the slice: x: 4, y: 4, z: 4, core: 2. Of those that a mesh axis runs over, the one named last changes fastest.
Arguments:
- tokens: bfloat16 [16384, 4096], P(('dp', 'mp')), may hold values from -6 to 6
- expert_ids: int32 [16384, 1], P(('dp', 'mp')), may hold values from 0 to 63; in each aligned block of 128 rows (0 to 127, 128 to 255, ...) at most 3 rows name the same one
- gate_probs: float32 [16384, 1], P(('dp', 'mp')), may hold values from 0.3 to 1
- gate_weight: bfloat16 [64, 4096, 1536], P('mp', None, 'dp'), may hold values from -0.09375 to 0.09375
- up_weight: bfloat16 [64, 4096, 1536], P('mp', None, 'dp'), may hold values from -0.09375 to 0.09375
- down_weight: bfloat16 [64, 1536, 4096], P('mp', 'dp'), may hold values from -0.15625 to 0.15625
- sign_offset: int32 [1], replicated, may hold values from 1 to 999999999
Outputs:
- out_plus: bfloat16 [16384, 4096], P(('dp', 'mp'))
- out_minus: bfloat16 [16384, 4096], P(('dp', 'mp'))
The draws below stay inside these ranges and needn't reach their ends.
Inputs may be any that keep to these rules, and one draw needn't show every extreme that they name: `expert_ids`: within each aligned block of 128 tokens (the tokens of one device) no expert is named by more than 3 routes, a bound that some block reaches.
All inputs are finite; a program needn't handle non-finite values.
Results may differ from the reference program's by a relative error of at most 0.01.
Values may be sent and summed in bfloat16 or wider, within the bound.
A program may use at most 128 MiB of HBM per device.

```python
import math
import jax
import jax.numpy as jnp
import numpy as np
from jax import lax

D = 4096
FF = 1536
TOP = 1
TOK_DEV = 128
EXPERTS = 64
TOKENS = 16384
CAP = 3
N_DP = 4


def level_of(key, shape, shards, least, largest):
    gain, own = 1.0, jax.random.fold_in(key, 6)
    for axis_at, parts in shards:
        draws = jnp.exp(jax.random.uniform(jax.random.fold_in(own, axis_at), (parts,), jnp.float32, least / len(shards), largest / len(shards)))
        gain = gain * jnp.repeat(draws, shape[axis_at] // parts).reshape([-1 if axis == axis_at else 1 for axis in range(len(shape))])
    return gain


def routed_block(rng, own, number, rows, number_of, top, most, skew):
    ranking = jax.random.permutation(rng, number_of)
    packed, usual = portions_of(number_of, rows * top, most, skew, True), portions_of(number_of, rows * top, most, skew, False)
    places = jnp.arange(number_of)

    def named(tallies, turn):
        used = int((tallies > 0).sum())
        fixed = max(1, used // 4)
        shifted = fixed + (places - fixed + turn * (used - fixed)) % max(1, number_of - fixed)
        return jnp.zeros((number_of,), jnp.int32).at[ranking[jnp.where(places < fixed, places, shifted)]].set(jnp.asarray(tallies, jnp.int32))

    tallies = jnp.where(number % 4 == 0, named(packed, number // 4), named(usual, number - number // 4 - 1))
    mixed = jax.random.permutation(jax.random.fold_in(own, 3), number_of)
    donor, receiver = mixed[0:number_of // 2 * 2:2], mixed[1:number_of // 2 * 2:2]
    room = jnp.minimum(tallies[donor] - 1, most - tallies[receiver]) // 2
    room = jnp.where((donor == ranking[0]) | (receiver == ranking[0]) | (tallies[receiver] == 0), 0, jnp.maximum(room, 0))
    shifted = jax.random.randint(jax.random.fold_in(own, 4), (number_of // 2,), 0, 1 << 20) % (room + 1)
    tallies = tallies.at[donor].add(-shifted).at[receiver].add(shifted)
    members = jnp.searchsorted(jnp.cumsum(tallies), jnp.arange(rows * top), side="right").astype(jnp.int32)
    grid = members.reshape(top, rows).T
    grid = grid[jax.random.permutation(jax.random.fold_in(own, 1), rows)]
    turn = jax.random.randint(jax.random.fold_in(own, 2), (rows, 1), 0, top)
    return jnp.take_along_axis(grid, (jnp.arange(top)[None, :] + turn) % top, axis=1)


def portions_of(count, total, most, skew, full):
    loads = [(1 << 20) // math.isqrt(standing ** skew) + 1 for standing in range(1, count + 1)]
    largest = most if full else min(most, max(-(-total // count), total * loads[0] // sum(loads)))
    least = 1 if total - largest >= count - 1 else 0
    counts, rest = [largest] + [least] * (count - 1), total - largest - least * (count - 1)
    while rest > 0:
        candidates = [i for i in range(1, count) if counts[i] < largest] or [i for i in range(1, count) if counts[i] < most]
        mass, left = sum([loads[i] for i in candidates]), rest
        for i in candidates:
            addition = min(most - counts[i], max(1, left * loads[i] // mass), rest)
            counts[i] = counts[i] + addition
            rest = rest - addition
    return np.array(counts)


def scatter_about(stream_key, dims, spread, bound, pieces=(), kind=jnp.bfloat16):
    drawn = jax.random.normal(stream_key, dims, jnp.float32) * spread
    if len(pieces) > 0:
        drawn = level_of(stream_key, dims, pieces, -0.22, 0.18) * drawn
    return jnp.clip(drawn, min=-bound, max=bound).astype(kind)


def setup_inputs(seed: int = 0) -> dict:
    seeds = jax.random.split(jax.random.key(seed), 8)
    tokens = scatter_about(seeds[0], (TOKENS, D), 1.0, 6.0, ((0, 128),))
    expert_ids_keys = jax.random.split(jax.random.fold_in(seeds[1], 1), TOKENS // TOK_DEV)
    expert_ids_turns = jax.random.permutation(jax.random.fold_in(seeds[1], 3), TOKENS // TOK_DEV)
    expert_ids = jax.vmap(lambda own, number: routed_block(jax.random.fold_in(seeds[1], 2), own, number, TOK_DEV, EXPERTS, TOP, CAP, 2))(expert_ids_keys, expert_ids_turns).reshape((TOKENS, TOP))
    gate_probs = jnp.clip(0.3 + 0.7 * jax.random.uniform(seeds[2], (TOKENS, TOP), jnp.float32) ** level_of(seeds[2], (TOKENS, TOP), ((0, 128),), -0.2, 0.2), 0.3, 1.0)
    gate_weight = scatter_about(seeds[3], (EXPERTS, D, FF), D ** -0.5, 0.09375, ((0, 32), (2, 4)))
    up_weight = scatter_about(seeds[4], (EXPERTS, D, FF), D ** -0.5, 0.09375, ((0, 32), (2, 4)))
    down_weight = scatter_about(seeds[5], (EXPERTS, FF, D), FF ** -0.5, 0.15625, ((0, 32), (1, 4)))
    sign_offset = jax.random.randint(seeds[6], (1,), 1, 1000000000).astype(jnp.int32)
    return {"tokens": tokens, "expert_ids": expert_ids, "gate_probs": gate_probs, "gate_weight": gate_weight, "up_weight": up_weight, "down_weight": down_weight, "sign_offset": sign_offset}


epsilon_step = 0.005


def mixing(number):
    number = number ^ lax.shift_right_logical(number, jnp.full_like(number, 16))
    number = number * 73244475
    number = number ^ lax.shift_right_logical(number, jnp.full_like(number, 16))
    number = number * 73244475
    return number ^ lax.shift_right_logical(number, jnp.full_like(number, 16))


def sign_noise(offset_mixed, position, matrix_tag):
    hashed = mixing((position * 3 + matrix_tag) ^ offset_mixed)
    parity = lax.shift_right_logical(hashed, jnp.full_like(hashed, 9)) & 1
    return (parity * 2 - 1).astype(jnp.float32)


def perturb(weight, noise, direction):
    return (weight.astype(jnp.float32) + direction * epsilon_step * noise).astype(jnp.bfloat16)


def reference(tokens, expert_ids, gate_probs, gate_weight, up_weight, down_weight, sign_offset):
    blocks = TOKENS // TOK_DEV
    per_block = TOK_DEV * TOP
    offset_mixed = mixing(sign_offset[0] * 668265261 + 12345)
    routes = expert_ids.reshape(blocks, per_block)
    expert_axis = jnp.arange(EXPERTS, dtype=jnp.int32)
    onehot = (routes[:, :, None] == expert_axis[None, None, :]).astype(jnp.int32)
    earlier = (jnp.cumsum(onehot, axis=1, dtype=jnp.int32) - onehot).astype(jnp.int32)
    rank_in = jnp.sum(earlier * onehot, axis=2, dtype=jnp.int32).astype(jnp.int32)
    block_axis = jnp.arange(blocks, dtype=jnp.int32)
    column = (routes * (blocks * CAP) + block_axis[:, None] * CAP + rank_in).reshape(-1).astype(jnp.int32)
    repeated = jnp.repeat(tokens, TOP, axis=0)
    buffer = jnp.zeros((EXPERTS * blocks * CAP, D), jnp.bfloat16).at[column].set(repeated)
    buffer = buffer.reshape(EXPERTS, blocks * CAP, D)
    width_axis = jnp.arange(D, dtype=jnp.int32)
    unit_axis = jnp.arange(FF, dtype=jnp.int32)
    quarter = FF // N_DP

    def one_expert(inputs):
        row_block, gate_one, up_one, down_one, expert = inputs
        gate_pos = (expert * D + width_axis[:, None]) * FF + unit_axis[None, :]
        down_pos = (expert * FF + unit_axis[:, None]) * D + width_axis[None, :]
        noise_gate = sign_noise(offset_mixed, gate_pos, 0)
        noise_up = sign_noise(offset_mixed, gate_pos, 1)
        noise_down = sign_noise(offset_mixed, down_pos, 2)
        results = []
        for direction in (1.0, -1.0):
            gate_moved = perturb(gate_one, noise_gate, direction)
            up_moved = perturb(up_one, noise_up, direction)
            down_moved = perturb(down_one, noise_down, direction)
            gate_act = jnp.dot(row_block, gate_moved, preferred_element_type=jnp.float32)
            up_act = jnp.dot(row_block, up_moved, preferred_element_type=jnp.float32)
            hidden = (jax.nn.silu(gate_act) * up_act).astype(jnp.bfloat16)
            running = jnp.zeros((row_block.shape[0], D), jnp.float32)
            for part_index in range(N_DP):
                first_unit = part_index * quarter
                partial_value = jnp.dot(hidden[:, first_unit:first_unit + quarter], down_moved[first_unit:first_unit + quarter], preferred_element_type=jnp.float32).astype(jnp.bfloat16)
                running = running + lax.optimization_barrier(partial_value).astype(jnp.float32)
            results.append(running.astype(jnp.bfloat16))
        return jnp.stack(results, axis=1)

    outputs = lax.map(one_expert, (buffer, gate_weight, up_weight, down_weight, expert_axis))
    flat_out = outputs.reshape(EXPERTS * blocks * CAP, 2, D)
    picked = jnp.take(flat_out, column, axis=0).reshape(TOKENS, TOP, 2, D).astype(jnp.float32)
    weighted = jnp.sum(gate_probs[:, :, None, None] * picked, axis=1)
    return weighted[:, 0].astype(jnp.bfloat16), weighted[:, 1].astype(jnp.bfloat16)
```

```python
import jax
import jax.numpy as jnp
from jax import lax
from jax.sharding import PartitionSpec as P

FF = 1536


epsilon_step = 0.005


def mixing(number):
    number = number ^ lax.shift_right_logical(number, jnp.full_like(number, 16))
    number = number * 73244475
    number = number ^ lax.shift_right_logical(number, jnp.full_like(number, 16))
    number = number * 73244475
    return number ^ lax.shift_right_logical(number, jnp.full_like(number, 16))


def sign_noise(offset_mixed, position, matrix_tag):
    hashed = mixing(position * 3 + matrix_tag ^ offset_mixed)
    parity = lax.shift_right_logical(hashed, jnp.full_like(hashed, 9)) & 1
    return (parity * 2 - 1).astype(jnp.float32)


def perturb(weight, noise, direction):
    return (weight.astype(jnp.float32) + direction * epsilon_step * noise).astype(jnp.bfloat16)


def expert_rows(arrived, weight_sets):
    lead_shape = arrived.shape
    model_width = lead_shape[-1]
    per_expert = []
    for local_expert in range(lead_shape[2]):
        flat_rows = arrived[:, :, local_expert].reshape(-1, model_width)
        by_pass = []
        for gate_moved, up_moved, down_moved in weight_sets[local_expert]:
            gate_act = jnp.dot(flat_rows, gate_moved, preferred_element_type=jnp.float32)
            up_act = jnp.dot(flat_rows, up_moved, preferred_element_type=jnp.float32)
            hidden = (jax.nn.silu(gate_act) * up_act).astype(jnp.bfloat16)
            by_pass.append(
                jnp.dot(hidden, down_moved, preferred_element_type=jnp.float32).astype(jnp.bfloat16)
            )
        stacked = jnp.stack(by_pass, axis=1).reshape(
            lead_shape[0], lead_shape[1], lead_shape[3], len(by_pass), model_width
        )
        per_expert.append(stacked)
    return jnp.stack(per_expert, axis=2)


def shards(tokens, expert_ids, gate_probs, gate_weight, up_weight, down_weight, sign_offset):
    mp_count = lax.axis_size("mp")
    tok_rows, model_width = tokens.shape
    route_count = expert_ids.shape[1]
    local_count = gate_weight.shape[0]
    quarter = gate_weight.shape[2]
    expert_count = local_count * mp_count
    capacity = 3 * tok_rows * route_count // (2 * expert_count)
    offset_mixed = mixing(sign_offset[0] * 668265261 + 12345)
    expert_base = lax.axis_index("mp") * local_count
    hidden_base = lax.axis_index("dp") * quarter
    width_axis = lax.broadcasted_iota(jnp.int32, (model_width, quarter), 0)
    unit_axis = lax.broadcasted_iota(jnp.int32, (model_width, quarter), 1) + hidden_base
    plus_sets = []
    minus_sets = []
    for local_expert in range(local_count):
        expert_global = expert_base + local_expert
        gate_pos = (expert_global * model_width + width_axis) * FF + unit_axis
        down_pos = (expert_global * FF + unit_axis.T) * model_width + width_axis.T
        noise_gate = sign_noise(offset_mixed, gate_pos, 0)
        noise_up = sign_noise(offset_mixed, gate_pos, 1)
        noise_down = sign_noise(offset_mixed, down_pos, 2)
        for direction, target in ((1.0, plus_sets), (-1.0, minus_sets)):
            target.append(
                (
                    perturb(gate_weight[local_expert], noise_gate, direction),
                    perturb(up_weight[local_expert], noise_up, direction),
                    perturb(down_weight[local_expert], noise_down, direction),
                )
            )
    route_flat = expert_ids.reshape(-1)
    expert_axis = lax.broadcasted_iota(jnp.int32, (route_flat.shape[0], expert_count), 1)
    onehot = (route_flat[:, None] == expert_axis).astype(jnp.int32)
    count = route_flat.shape[0]
    before = lax.broadcasted_iota(jnp.int32, (count, count), 1) < lax.broadcasted_iota(
        jnp.int32, (count, count), 0
    )
    alike = route_flat[:, None] == route_flat[None, :]
    rank_in = jnp.sum((before & alike).astype(jnp.int32), axis=1, dtype=jnp.int32)
    slot_of = (route_flat * capacity + rank_in).reshape(tok_rows, route_count)
    slot_axis = lax.broadcasted_iota(jnp.int32, (expert_count * capacity, tok_rows), 0)
    selector = (slot_axis == slot_of[:, 0][None, :]).astype(jnp.float32)
    outgoing = jnp.dot(
        selector.astype(jnp.bfloat16), tokens, preferred_element_type=jnp.float32
    ).astype(jnp.bfloat16)
    outgoing = outgoing.reshape(mp_count, local_count, capacity, model_width)
    exchanged = lax.all_to_all(outgoing, "mp", split_axis=0, concat_axis=0, tiled=True)
    arrived = lax.all_gather(exchanged[None], "dp", axis=0, tiled=True)

    def finish(weight_sets):
        partials = expert_rows(arrived, weight_sets)
        summed = lax.psum_scatter(partials, "dp", scatter_dimension=0, tiled=True)
        return lax.all_to_all(summed[0], "mp", split_axis=0, concat_axis=0, tiled=True)

    def combine(result, pass_index):
        flat_out = result.reshape(expert_count * capacity, result.shape[3], model_width)[
            :, pass_index
        ]
        picked = (
            jnp.take(flat_out, slot_of.reshape(-1), axis=0)
            .reshape(tok_rows, route_count, model_width)
            .astype(jnp.float32)
        )
        return jnp.sum(gate_probs[:, :, None] * picked, axis=1).astype(jnp.bfloat16)

    plus_result = finish([[entry_set] for entry_set in plus_sets])
    minus_result = finish([[entry_set] for entry_set in minus_sets])
    return (combine(plus_result, 0), combine(minus_result, 0))


def solution(mesh):
    in_specs = (
        P(("dp", "mp"), None),
        P(("dp", "mp"), None),
        P(("dp", "mp"), None),
        P("mp", None, "dp"),
        P("mp", None, "dp"),
        P("mp", "dp", None),
        P(),
    )
    out_specs = (P(("dp", "mp"), None), P(("dp", "mp"), None))
    return jax.shard_map(shards, mesh=mesh, in_specs=in_specs, out_specs=out_specs, check_vma=False)
```

```python
import jax
import jax.numpy as jnp
import numpy as np
from jax import lax
from jax.experimental import pallas as pl
from jax.experimental.pallas import tpu as pltpu
from jax.sharding import PartitionSpec as P

D = 4096
FF = 1536
Q = 384
CAP = 3
ROWS = 96
HALF = 48
MSG = 48
PEERS = 32
EPS = 0.005
MESH = pl.DeviceIdType.MESH
F32, BF16, I32 = jnp.float32, jnp.bfloat16, jnp.int32


def mixing(number):
    number = number ^ lax.shift_right_logical(number, jnp.full_like(number, 16))
    number = number * 73244475
    number = number ^ lax.shift_right_logical(number, jnp.full_like(number, 16))
    number = number * 73244475
    return number ^ lax.shift_right_logical(number, jnp.full_like(number, 16))


def moved_by(position, offset_mixed):
    hashed = mixing(position ^ offset_mixed)
    return jnp.where((hashed & 512) != 0, EPS, -EPS).astype(F32)


def kernel(
    ids_row, ids_col, probs, sign_offset, swap, slots_col, slots_row, tokens, gate_w, up_w, down_w,
    out_plus, out_minus,
    rows, sent, came, wide, down, part, relay, home, back, acc, hidden, perm,
    w_sem, a_send, a_recv, z_send, z_recv, p_send, r_recv, h_recv, b_send, b_recv, o_sem,
):
    z, m = lax.axis_index("dp"), lax.axis_index("mp")
    x, y, core = m // 8, (m // 2) % 4, m % 2
    above, below = (z + 1) % 4, (z + 3) % 4
    hidden_base = z * Q

    def peer(p, sign):
        return (
            (x + sign * (p // 8) + 4) % 4 * 8
            + (y + sign * ((p // 2) % 4) + 4) % 4 * 2
            + (core + p) % 2
        )

    def load_weights(e):
        for i, (source, target) in enumerate(
            (
                (gate_w, wide.at[0, :, 0:Q]),
                (up_w, wide.at[0, :, Q : 2 * Q]),
                (down_w, down.at[0]),
            )
        ):
            yield pltpu.make_async_copy(source.at[e], target, w_sem.at[i])

    for copy in load_weights(0):
        copy.start()

    barrier = pltpu.get_barrier_semaphore()

    @pl.loop(1, PEERS)
    def _(p):
        pl.semaphore_signal(barrier, inc=1, device_id=(z, peer(p, -1)), device_id_type=MESH)

    for near in (above, below):
        pl.semaphore_signal(barrier, inc=1, device_id=(near, m), device_id_type=MESH)
    pl.semaphore_wait(barrier, PEERS + 1)

    alike = ids_col[...] == ids_row[...]
    at_row = lax.broadcasted_iota(I32, (128, 128), 0)
    at_col = lax.broadcasted_iota(I32, (128, 128), 1)
    key_col = ids_col[...] * 4 + jnp.sum(
        jnp.where(alike & (at_col < at_row), 1, 0), axis=1, keepdims=True
    )
    key_row = ids_row[...] * 4 + jnp.sum(
        jnp.where(alike & (at_row < at_col), 1, 0), axis=0, keepdims=True
    )

    def slot_keys(a, b, d, s, e):
        owner = ((x - a) & 3) * 8 + ((y - b) & 3) * 2 + ((core + d) & 1)
        return (owner * 2 + e) * 4 + s

    perm[...] = jnp.where(
        lax.broadcasted_iota(I32, (768, 768), 1) == swap[...], 1.0, 0.0
    ).astype(BF16)

    def pack(source, target, i, half):
        stacked = jnp.concatenate(
            [
                source[half * HALF : (half + 1) * HALF, c * 256 : (c + 1) * 256]
                for c in range(16)
            ],
            axis=0,
        )
        target[i, half * 768 : (half + 1) * 768, :] = jnp.dot(
            perm[...], stacked, preferred_element_type=F32
        ).astype(BF16)

    def unpack(source, i, half, target):
        laid = jnp.dot(
            perm[...], source[i, half * 768 : (half + 1) * 768, :], preferred_element_type=F32
        ).astype(BF16)
        for c in range(16):
            target[half * HALF : (half + 1) * HALF, c * 256 : (c + 1) * 256] = laid[
                c * HALF : (c + 1) * HALF
            ]

    def exchange(i, target, j, sign, half, send_sem, recv_sem):
        @pl.loop(max(1, half * 16), half * 16 + 16)
        def _(p):
            at = pl.ds(pl.multiple_of(p * MSG, MSG), MSG)
            pltpu.make_async_remote_copy(
                sent.at[i, at], target.at[j, at], send_sem, recv_sem,
                device_id=(z, peer(p, sign)), device_id_type=MESH,
            ).start()

    def whole(i, target, j, lo, hi, send_sem, recv_sem):
        return pltpu.make_async_remote_copy(
            sent.at[i, lo:hi], target.at[j, lo:hi], send_sem, recv_sem,
            device_id=(z, peer(1, 1)), device_id_type=MESH,
        )

    for e in range(2):
        chosen = jnp.where(
            key_row == slot_keys(*[slots_col[:, i : i + 1] for i in range(4)], e), 1.0, 0.0
        ).astype(BF16)
        staged = part.at[0, e]
        for c in range(4):
            cols = slice(c * 1024, (c + 1) * 1024)
            staged[0:ROWS, cols] = jnp.dot(
                chosen, tokens[:, cols], preferred_element_type=F32
            ).astype(BF16)
        for half in range(2):
            pack(staged, sent, e, half)
            exchange(e, came, e, -1, half, a_send.at[e], a_recv.at[e, half])
        came[e, 0:MSG, :] = sent[e, 0:MSG, :]

    offset_mixed = mixing(sign_offset[0] * 668265261 + 12345)

    def move_wide(e, lo, hi):
        expert = m * 2 + e
        inner = lax.broadcasted_iota(I32, (32, Q), 0) * (3 * FF) + lax.broadcasted_iota(
            I32, (32, Q), 1
        ) * 3

        @pl.loop(lo, hi)
        def _(i):
            at = pl.ds(pl.multiple_of(i * 32, 32), 32)
            first = ((expert * D + i * 32) * FF + hidden_base) * 3
            for tag in range(2):
                cols = slice(tag * Q, (tag + 1) * Q)
                weight = wide[0, at, cols].astype(F32)
                step = moved_by(inner + (first + tag), offset_mixed)
                wide[0, at, cols] = (weight + step).astype(BF16)
                wide[1, at, cols] = (weight - step).astype(BF16)

    def move_down(e, lo, hi):
        expert = m * 2 + e
        inner = lax.broadcasted_iota(I32, (32, 512), 0) * (3 * D) + lax.broadcasted_iota(
            I32, (32, 512), 1
        ) * 3

        @pl.loop(lo, hi)
        def _(i):
            row, col = i // 8 * 32, i % 8 * 512
            at, cols = pl.ds(pl.multiple_of(row, 32), 32), pl.ds(pl.multiple_of(col, 512), 512)
            first = ((expert * FF + hidden_base + row) * D + col) * 3 + 2
            weight = down[0, at, cols].astype(F32)
            step = moved_by(inner + first, offset_mixed)
            down[0, at, cols] = (weight + step).astype(BF16)
            down[1, at, cols] = (weight - step).astype(BF16)

    def gather_copy(e, from_slot, to_slot, half, n, to):
        return pltpu.make_async_remote_copy(
            rows.at[e, from_slot * ROWS + half * HALF : from_slot * ROWS + (half + 1) * HALF],
            rows.at[e, to_slot * ROWS + half * HALF : to_slot * ROWS + (half + 1) * HALF],
            z_send.at[e, n], z_recv.at[e, to_slot, half],
            device_id=(to, m), device_id_type=MESH,
        )

    def gather_up(e, half):
        return gather_copy(e, 0, 1, half, half, above)

    def gather_down(e, half):
        return gather_copy(e, 0, 2, half, 2 + half, below)

    def gather_on(e, half):
        return gather_copy(e, 1 + half, 3, half, 4 + half, (above, below)[half])

    def arrive(e, half):
        lo, hi = max(1, half * 16) * MSG, (half + 1) * 16 * MSG
        whole(e, came, e, lo, hi, a_send.at[e], a_recv.at[e, half]).wait_recv()
        unpack(came, e, half, rows.at[e, 0:ROWS])
        gather_up(e, half).start()
        gather_down(e, half).start()

    def pass_on(e):
        gather_up(e, 0).wait_recv()
        gather_on(e, 0).start()
        gather_down(e, 1).wait_recv()
        gather_on(e, 1).start()

    def gathered(e):
        gather_up(e, 1).wait_recv()
        gather_down(e, 0).wait_recv()
        for half in range(2):
            gather_on(e, half).wait_recv()

    def multiply(e, s):
        acc[...] = jnp.zeros_like(acc)

        @pl.loop(0, 8)
        def _(k):
            at = pl.ds(pl.multiple_of(k * 512, 512), 512)
            acc[...] += jnp.dot(rows[e, :, at], wide[s, at, :], preferred_element_type=F32)

        @pl.loop(0, 8)
        def _(i):
            at = pl.ds(pl.multiple_of(i * HALF, HALF), HALF)
            gate = acc[at, 0:Q]
            hidden[at, :] = (gate / (1.0 + jnp.exp(-gate)) * acc[at, Q : 2 * Q]).astype(BF16)

        @pl.loop(0, 8)
        def _(j):
            cols = pl.ds(pl.multiple_of(j * 512, 512), 512)
            part[e, s, :, cols] = jnp.dot(
                hidden[...], down[s, :, cols], preferred_element_type=F32
            ).astype(BF16)

    def at_part(e, s, slot, half):
        return part.at[e, s, slot * ROWS + half * HALF : slot * ROWS + (half + 1) * HALF]

    def copy_back(e, s, which):
        def to(source, target, n, recv_sem, device):
            return pltpu.make_async_remote_copy(
                source, target, p_send.at[e, s, n], recv_sem,
                device_id=(device, m), device_id_type=MESH,
            )

        def at_relay(k):
            return relay.at[e, s, k * HALF : (k + 1) * HALF]

        def at_home(k, half):
            return home.at[e, s, k, half * HALF : (half + 1) * HALF]

        if which < 2:
            half, device = which, (below, above)[which]
            return to(at_part(e, s, 3, half), at_relay(half), which, r_recv.at[e, s, half], device)
        k, half = ((0, 1), (1, 0), (0, 0), (1, 1))[which - 2]
        return to(
            at_part(e, s, 1 + k, half), at_home(k, half), which, h_recv.at[e, s, k, half],
            (below, above)[k],
        )

    def start_back(e, s):
        for which in range(4):
            copy_back(e, s, which).start()

    def relay_back(e, s):
        for k in range(2):
            copy_back(e, s, k).wait_recv()
            first = (1 + k) * ROWS + k * HALF

            @pl.loop(0, 8)
            def _(j):
                cols = pl.ds(pl.multiple_of(j * 512, 512), 512)
                part[e, s, first : first + HALF, cols] = (
                    part[e, s, first : first + HALF, cols].astype(F32)
                    + relay[e, s, k * HALF : (k + 1) * HALF, cols].astype(F32)
                ).astype(BF16)

            copy_back(e, s, 4 + k).start()

    def finish_back(e, s):
        for which in range(2, 6):
            copy_back(e, s, which).wait_recv()

        @pl.loop(0, 8)
        def _(j):
            cols = pl.ds(pl.multiple_of(j * 512, 512), 512)
            part[e, s, 0:ROWS, cols] = (
                part[e, s, 0:ROWS, cols].astype(F32)
                + home[e, s, 0, :, cols].astype(F32)
                + home[e, s, 1, :, cols].astype(F32)
            ).astype(BF16)

        i = 2 * e + s
        for half in range(2):
            pack(part.at[e, s], sent, i, half)
            exchange(i, back, i, 1, half, b_send.at[i], b_recv.at[i])
        back[i, 0:MSG, :] = sent[i, 0:MSG, :]

    loads = list(load_weights(0))
    loads[0].wait()
    loads[1].wait()
    move_wide(0, 0, 32)
    arrive(0, 0)
    arrive(0, 1)
    move_wide(0, 32, 96)
    pass_on(0)
    arrive(1, 0)
    arrive(1, 1)
    move_wide(0, 96, 128)
    loads[2].wait()
    move_down(0, 0, 96)
    gathered(0)
    multiply(0, 0)
    start_back(0, 0)
    multiply(0, 1)
    start_back(0, 1)
    for e in range(2):
        whole(e, came, e, MSG, PEERS * MSG, a_send.at[e], a_recv.at[e, 0]).wait_send()
    loads = list(load_weights(1))
    for copy in loads:
        copy.start()
    pass_on(1)
    loads[0].wait()
    loads[1].wait()
    move_wide(1, 0, 64)
    relay_back(0, 0)
    move_wide(1, 64, 128)
    loads[2].wait()
    relay_back(0, 1)
    move_down(1, 0, 96)
    gathered(1)
    multiply(1, 0)
    start_back(1, 0)
    multiply(1, 1)
    start_back(1, 1)
    finish_back(0, 0)
    finish_back(0, 1)
    relay_back(1, 0)
    relay_back(1, 1)
    finish_back(1, 0)
    finish_back(1, 1)

    for e in range(2):
        for half in range(2):
            for copy in (gather_up(e, half), gather_down(e, half), gather_on(e, half)):
                copy.wait_send()
        for s in range(2):
            for which in range(6):
                copy_back(e, s, which).wait_send()

    chosen = [
        jnp.where(
            key_col == slot_keys(*[slots_row[i : i + 1, :] for i in range(4)], e), 1.0, 0.0
        ).astype(BF16)
        for e in range(2)
    ]
    for s in range(2):
        for e in range(2):
            i = 2 * e + s
            whole(i, back, i, MSG, PEERS * MSG, b_send.at[i], b_recv.at[i]).wait()
            for half in range(2):
                unpack(back, i, half, part.at[e, s])

        @pl.loop(0, 4)
        def _(j):
            cols = pl.ds(pl.multiple_of(j * 1024, 1024), 1024)
            picked = jnp.dot(
                chosen[0], part[0, s, 0:ROWS, cols], preferred_element_type=F32
            ) + jnp.dot(chosen[1], part[1, s, 0:ROWS, cols], preferred_element_type=F32)
            part[0, s, ROWS : ROWS + 128, cols] = (probs[...] * picked).astype(BF16)

        target = (out_plus, out_minus)[s]
        pltpu.make_async_copy(part.at[0, s, ROWS : ROWS + 128], target, o_sem.at[s]).start()
    for s in range(2):
        target = (out_plus, out_minus)[s]
        pltpu.make_async_copy(part.at[0, s, ROWS : ROWS + 128], target, o_sem.at[s]).wait()


def shards(tokens, expert_ids, gate_probs, gate_weight, up_weight, down_weight, sign_offset):
    at = np.arange(768)
    swap = (at % 48 // 3 * 48 + at // 48 * 3 + at % 3).astype(np.int32).reshape(768, 1)
    slot = np.arange(ROWS)
    peer = slot // CAP
    slots = np.stack([peer // 8, peer // 2 % 4, peer % 2, slot % CAP], axis=1).astype(np.int32)
    vmem, hbm = pl.BlockSpec(memory_space=pltpu.VMEM), pl.BlockSpec(memory_space=pl.ANY)
    smem = pl.BlockSpec(memory_space=pltpu.SMEM)
    dma = pltpu.SemaphoreType.DMA
    return pl.pallas_call(
        kernel,
        out_shape=[jax.ShapeDtypeStruct((128, D), BF16)] * 2,
        in_specs=[vmem, vmem, vmem, smem, vmem, vmem, vmem, vmem, hbm, hbm, hbm],
        out_specs=[hbm, hbm],
        scratch_shapes=[
            pltpu.VMEM((2, 4 * ROWS, D), BF16),
            pltpu.VMEM((4, PEERS * MSG, 256), BF16),
            pltpu.VMEM((2, PEERS * MSG, 256), BF16),
            pltpu.VMEM((2, D, 2 * Q), BF16),
            pltpu.VMEM((2, Q, D), BF16),
            pltpu.VMEM((2, 2, 4 * ROWS, D), BF16),
            pltpu.VMEM((2, 2, ROWS, D), BF16),
            pltpu.VMEM((2, 2, 2, ROWS, D), BF16),
            pltpu.VMEM((4, PEERS * MSG, 256), BF16),
            pltpu.VMEM((4 * ROWS, 2 * Q), F32),
            pltpu.VMEM((4 * ROWS, Q), BF16),
            pltpu.VMEM((768, 768), BF16),
            dma((3,)),
            dma((2,)),
            dma((2, 2)),
            dma((2, 6)),
            dma((2, 4, 2)),
            dma((2, 2, 6)),
            dma((2, 2, 2)),
            dma((2, 2, 2, 2)),
            dma((4,)),
            dma((4,)),
            dma((2,)),
        ],
        compiler_params=pltpu.CompilerParams(
            collective_id=0, has_side_effects=True, vmem_limit_bytes=63_000_000
        ),
    )(
        expert_ids.reshape(1, 128),
        expert_ids,
        gate_probs,
        sign_offset,
        jnp.asarray(swap),
        jnp.asarray(slots),
        jnp.asarray(slots.T),
        tokens,
        gate_weight,
        up_weight,
        down_weight,
    )


def solution(mesh):
    in_specs = (
        P(("dp", "mp"), None),
        P(("dp", "mp"), None),
        P(("dp", "mp"), None),
        P("mp", None, "dp"),
        P("mp", None, "dp"),
        P("mp", "dp", None),
        P(),
    )
    out_specs = (P(("dp", "mp"), None), P(("dp", "mp"), None))
    return jax.shard_map(shards, mesh=mesh, in_specs=in_specs, out_specs=out_specs, check_vma=False)
```

```python
import jax
import jax.numpy as jnp
import numpy as np
from jax import lax
from jax.experimental import pallas as pl
from jax.experimental.pallas import tpu as pltpu
from jax.sharding import PartitionSpec as P

D = 4096
FF = 1536
Q = 384
CAP = 3
ROWS = 96
HALF = 48
WIDTH = 2048
MSG = 48
PEERS = 32
EPS = 0.005
MESH = pl.DeviceIdType.MESH
F32, BF16, I32 = jnp.float32, jnp.bfloat16, jnp.int32


def mixing(number):
    number = number ^ lax.shift_right_logical(number, jnp.full_like(number, 16))
    number = number * 73244475
    number = number ^ lax.shift_right_logical(number, jnp.full_like(number, 16))
    number = number * 73244475
    return number ^ lax.shift_right_logical(number, jnp.full_like(number, 16))


def moved_by(position, offset_mixed):
    hashed = mixing(position ^ offset_mixed)
    return jnp.where((hashed & 512) != 0, EPS, -EPS).astype(F32)


def kernel(
    ids_row, probs_row, sign_offset, swap, slots_col, slots_row, tokens, gate_w, up_w, down_w,
    out_plus, out_minus,
    ids_all, others, rows, sent_t, came_t, back_t, sent_s, came_s, back_s, wide, down, part_t, part_s,
    relay_s, home_s, relay_t, home_t, acc, hidden, perm,
    w_sem, i_send, i_recv, t_send, t_recv, xs_send, xs_recv, xt_send, xt_recv, z_send, z_recv,
    ps_send, rs_recv, hs_recv, pt_send, rt_recv, ht_recv, bs_send, bs_recv, bt_send, bt_recv, o_sem,
    free_sem,
):
    z, m = lax.axis_index("dp"), lax.axis_index("mp")
    x, y, core = m // 8, (m // 2) % 4, m % 2
    above, below, across = (z + 1) % 4, (z + 3) % 4, (z + 2) % 4
    hidden_base = z * Q

    def peer(p, sign):
        return (
            (x + sign * (p // 8) + 4) % 4 * 8
            + (y + sign * ((p // 2) % 4) + 4) % 4 * 2
            + (core + p) % 2
        )

    def remote(source, target, send_sem, recv_sem, device):
        return pltpu.make_async_remote_copy(
            source, target, send_sem, recv_sem, device_id=device, device_id_type=MESH
        )

    def load_weights(e):
        return [
            pltpu.make_async_copy(source.at[e], target, w_sem.at[i])
            for i, (source, target) in enumerate(
                (
                    (gate_w, wide.at[0, :, 0:Q]),
                    (up_w, wide.at[0, :, Q : 2 * Q]),
                    (down_w, down.at[0]),
                )
            )
        ]

    loads = load_weights(0)
    for copy in loads:
        copy.start()

    barrier = pltpu.get_barrier_semaphore()

    @pl.loop(1, PEERS)
    def _(p):
        pl.semaphore_signal(barrier, inc=1, device_id=(z, peer(p, -1)), device_id_type=MESH)

    for near in (above, below, across):
        pl.semaphore_signal(barrier, inc=1, device_id=(near, m), device_id_type=MESH)
    ids_all[0] = jnp.broadcast_to(ids_row[...], (8, 128))
    pl.semaphore_wait(barrier, PEERS + 2)

    def token_copy(up, half):
        at = slice(half * 64, half * 64 + 64)
        return remote(
            tokens.at[at, 0:WIDTH], others.at[0 if up else 1, at], t_send.at[0 if up else 1, half],
            t_recv.at[0 if up else 1, half], (above if up else below, m),
        )

    def token_on(half):
        at = slice(half * 64, half * 64 + 64)
        return remote(
            others.at[half, at], others.at[2, at], t_send.at[2, half], t_recv.at[2, half],
            ((above, below)[half], m),
        )

    def id_copy(slot):
        device = (above, below, across)[slot - 1]
        return remote(
            ids_all.at[0], ids_all.at[slot], i_send.at[slot - 1], i_recv.at[slot - 1], (device, m)
        )

    for slot in (1, 2, 3):
        id_copy(slot).start()
    for half in range(2):
        token_copy(True, half).start()
        token_copy(False, 1 - half).start()

    at_row = lax.broadcasted_iota(I32, (128, 128), 0)
    at_col = lax.broadcasted_iota(I32, (128, 128), 1)

    def as_column(row):
        return jnp.sum(jnp.where(at_row == at_col, row, jnp.zeros_like(row)), axis=1, keepdims=True)

    def keys(slot):
        row = ids_all[slot][0:1]
        column = as_column(row)
        alike = column == row
        key_col = column * 4 + jnp.sum(
            jnp.where(alike & (at_col < at_row), 1, 0), axis=1, keepdims=True
        )
        key_row = row * 4 + jnp.sum(
            jnp.where(alike & (at_row < at_col), 1, 0), axis=0, keepdims=True
        )
        return key_col, key_row

    def slot_keys(a, b, d, s, e):
        owner = ((x - a) & 3) * 8 + ((y - b) & 3) * 2 + ((core + d) & 1)
        return (owner * 2 + e) * 4 + s

    def one_hot(found):
        return jnp.where(found, 1.0, 0.0).astype(BF16)

    def to_slots(key_row, e):
        return one_hot(key_row == slot_keys(*[slots_col[:, i : i + 1] for i in range(4)], e))

    def to_tokens(key_col, e):
        return one_hot(key_col == slot_keys(*[slots_row[i : i + 1, :] for i in range(4)], e))

    perm[...] = one_hot(lax.broadcasted_iota(I32, (768, 768), 1) == swap[...])

    def swapped(value):
        return jnp.dot(perm[...], value, preferred_element_type=F32).astype(BF16)

    def piece(ref, slot, half, c):
        first = slot * ROWS + half * HALF
        return ref[first : first + HALF, c * 128 : (c + 1) * 128]

    def pack_s(source, target):
        laid = swapped(
            jnp.concatenate(
                [
                    jnp.concatenate([piece(source, 0, half, c) for half in range(2)], axis=1)
                    for c in range(16)
                ],
                axis=0,
            )
        )
        for half in range(2):
            target[half * 768 : (half + 1) * 768, :] = laid[:, half * 128 : (half + 1) * 128]

    def unpack_s(source, target, left):
        laid = swapped(jnp.concatenate([source[0:768, :], source[768:1536, :]], axis=1))
        for half in range(2):
            for c in range(16):
                target[
                    half * HALF : (half + 1) * HALF, left + c * 128 : left + (c + 1) * 128
                ] = laid[c * HALF : (c + 1) * HALF, half * 128 : (half + 1) * 128]

    def pack_t(source, target):
        for half in range(2):
            target[half * 768 : (half + 1) * 768, :] = swapped(
                jnp.concatenate(
                    [
                        jnp.concatenate([piece(source, slot, half, c) for slot in range(4)], axis=1)
                        for c in range(16)
                    ],
                    axis=0,
                )
            )

    def unpack_t(source, target, left):
        for half in range(2):
            laid = swapped(source[half * 768 : (half + 1) * 768, :])
            for slot in range(4):
                for c in range(16):
                    first = slot * ROWS + half * HALF
                    target[first : first + HALF, left + c * 128 : left + (c + 1) * 128] = laid[
                        c * HALF : (c + 1) * HALF, slot * 128 : (slot + 1) * 128
                    ]

    def exchange(source, target, send_sem, recv_sem, sign):
        @pl.loop(1, PEERS)
        def _(p):
            at = pl.ds(pl.multiple_of(p * MSG, MSG), MSG)
            remote(
                source.at[at], target.at[at], send_sem, recv_sem, (z, peer(p, sign))
            ).start()

        target[0:MSG, :] = source[0:MSG, :]

    def exchanged(source, target, send_sem, recv_sem):
        return remote(
            source.at[MSG : PEERS * MSG], target.at[MSG : PEERS * MSG], send_sem, recv_sem,
            (z, peer(1, 1)),
        )

    def out_s(e):
        return sent_s.at[e], came_s.at[e], xs_send.at[e], xs_recv.at[e]

    def out_t(e):
        return sent_t.at[e], came_t.at[e], xt_send.at[e], xt_recv.at[e]

    def home_of(e, s, sent, came, back, send_sem, recv_sem):
        i = 2 * e + s
        if e == 0:
            return sent.at[2 + s], back.at[s], send_sem.at[i], recv_sem.at[i]
        return sent.at[s], came.at[s], send_sem.at[i], recv_sem.at[i]

    def in_s(e, s):
        return home_of(e, s, sent_s, came_s, back_s, bs_send, bs_recv)

    def in_t(e, s):
        return home_of(e, s, sent_t, came_t, back_t, bt_send, bt_recv)

    key = [keys(0)]
    for e in range(2):
        chosen = to_slots(key[0][1], e)
        staged = part_s.at[0, e]
        for c in range(2):
            staged[0:ROWS, c * 1024 : (c + 1) * 1024] = jnp.dot(
                chosen,
                tokens[:, WIDTH + c * 1024 : WIDTH + (c + 1) * 1024],
                preferred_element_type=F32,
            ).astype(BF16)
        pack_s(staged, sent_s.at[e])
        exchange(*out_s(e), -1)

    offset_mixed = mixing(sign_offset[0] * 668265261 + 12345)

    def move_wide(e, lo, hi):
        expert = m * 2 + e
        inner = lax.broadcasted_iota(I32, (32, Q), 0) * (3 * FF) + lax.broadcasted_iota(
            I32, (32, Q), 1
        ) * 3

        @pl.loop(lo, hi)
        def _(i):
            at = pl.ds(pl.multiple_of(i * 32, 32), 32)
            first = ((expert * D + i * 32) * FF + hidden_base) * 3
            for tag in range(2):
                cols = slice(tag * Q, (tag + 1) * Q)
                weight = wide[0, at, cols].astype(F32)
                step = moved_by(inner + (first + tag), offset_mixed)
                wide[0, at, cols] = (weight + step).astype(BF16)
                wide[1, at, cols] = (weight - step).astype(BF16)

    def move_down(e, lo, hi):
        expert = m * 2 + e
        inner = lax.broadcasted_iota(I32, (32, 512), 0) * (3 * D) + lax.broadcasted_iota(
            I32, (32, 512), 1
        ) * 3

        @pl.loop(lo, hi)
        def _(i):
            row, col = i // 8 * 32, i % 8 * 512
            at, cols = pl.ds(pl.multiple_of(row, 32), 32), pl.ds(pl.multiple_of(col, 512), 512)
            first = ((expert * FF + hidden_base + row) * D + col) * 3 + 2
            weight = down[0, at, cols].astype(F32)
            step = moved_by(inner + first, offset_mixed)
            down[0, at, cols] = (weight + step).astype(BF16)
            down[1, at, cols] = (weight - step).astype(BF16)

    def tokens_on():
        token_copy(True, 0).wait_recv()
        token_on(0).start()
        token_copy(False, 1).wait_recv()
        token_on(1).start()

    def tokens_there():
        token_copy(True, 1).wait_recv()
        token_copy(False, 0).wait_recv()
        for half in range(2):
            token_on(half).wait_recv()
        for slot in (1, 2, 3):
            id_copy(slot).wait_recv()
            key.append(keys(slot))

    def dispatch_t(e):
        for slot in range(4):
            chosen = to_slots(key[slot][1], e)
            for c in range(2):
                cols = slice(c * 1024, (c + 1) * 1024)
                value = tokens[:, cols] if slot == 0 else others[slot - 1, :, cols]
                part_t[slot * ROWS : (slot + 1) * ROWS, cols] = jnp.dot(
                    chosen, value, preferred_element_type=F32
                ).astype(BF16)
        pack_t(part_t, sent_t.at[e])
        exchange(*out_t(e), -1)

    def arrive_t(e):
        exchanged(*out_t(e)).wait_recv()
        unpack_t(came_t.at[e], rows.at[e], 0)

    def arrive_s(e):
        exchanged(*out_s(e)).wait_recv()
        unpack_s(came_s.at[e], rows.at[e], WIDTH)

    def gather_copy(e, from_slot, to_slot, half, n, to):
        a, b = from_slot * ROWS + half * HALF, to_slot * ROWS + half * HALF
        return remote(
            rows.at[e, a : a + HALF, WIDTH:D], rows.at[e, b : b + HALF, WIDTH:D],
            z_send.at[e, n], z_recv.at[e, to_slot, half], (to, m),
        )

    def gather_up(e, half):
        return gather_copy(e, 0, 1, half, half, above)

    def gather_down(e, half):
        return gather_copy(e, 0, 2, half, 2 + half, below)

    def gather_on(e, half):
        return gather_copy(e, 1 + half, 3, half, 4 + half, (above, below)[half])

    def gather(e):
        for half in range(2):
            gather_up(e, half).start()
            gather_down(e, 1 - half).start()

    def pass_on(e):
        gather_up(e, 0).wait_recv()
        gather_on(e, 0).start()
        gather_down(e, 1).wait_recv()
        gather_on(e, 1).start()

    def gathered(e):
        gather_up(e, 1).wait_recv()
        gather_down(e, 0).wait_recv()
        for half in range(2):
            gather_on(e, half).wait_recv()

    def ring(block, relay, home, send_sem, relay_sem, home_sem):
        def copy(which):
            if which < 2:
                half = which
                return remote(
                    block(3, half), relay(half), send_sem.at[which], relay_sem.at[half],
                    ((below, above)[half], m),
                )
            k, half = ((0, 1), (1, 0), (0, 0), (1, 1))[which - 2]
            return remote(
                block(1 + k, half), home(k, half), send_sem.at[which], home_sem.at[k, half],
                ((below, above)[k], m),
            )

        def start():
            for which in range(4):
                copy(which).start()

        def pass_sum():
            for k in range(2):
                copy(k).wait_recv()
                mine, arrived = block(1 + k, k), relay(k)

                @pl.loop(0, 4)
                def _(j):
                    cols = pl.ds(pl.multiple_of(j * 512, 512), 512)
                    mine[:, cols] = (
                        mine[:, cols].astype(F32) + arrived[:, cols].astype(F32)
                    ).astype(BF16)

                copy(4 + k).start()

        def wait_home():
            for which in range(2, 6):
                copy(which).wait_recv()

        def wait_sent():
            for which in range(6):
                copy(which).wait_send()

        return start, pass_sum, wait_home, wait_sent

    def ring_s(e, s):
        def block(slot, half):
            return part_s.at[e, s, slot * ROWS + half * HALF : slot * ROWS + (half + 1) * HALF]

        return ring(
            block,
            lambda half: relay_s.at[e, s, half * HALF : (half + 1) * HALF],
            lambda k, half: home_s.at[e, s, k, half * HALF : (half + 1) * HALF],
            ps_send.at[e, s], rs_recv.at[e, s], hs_recv.at[e, s],
        )

    def block_t(s, slot, lo, hi):
        top, left = slot // 2 * 128, slot % 2 * WIDTH
        return down.at[s, top + lo : top + hi, left : left + WIDTH]

    def ring_t(s):
        return ring(
            lambda slot, half: block_t(s, slot, half * 64, half * 64 + 64),
            lambda half: relay_t.at[s, half * 64 : half * 64 + 64],
            lambda k, half: home_t.at[s, k, half * 64 : half * 64 + 64],
            pt_send.at[s], rt_recv.at[s], ht_recv.at[s],
        )

    def multiply(e, s):
        acc[...] = jnp.zeros_like(acc)

        @pl.loop(0, 8)
        def _(k):
            at = pl.ds(pl.multiple_of(k * 512, 512), 512)
            acc[...] += jnp.dot(rows[e, :, at], wide[s, at, :], preferred_element_type=F32)

        @pl.loop(0, 8)
        def _(i):
            at = pl.ds(pl.multiple_of(i * HALF, HALF), HALF)
            gate = acc[at, 0:Q]
            hidden[at, :] = (gate / (1.0 + jnp.exp(-gate)) * acc[at, Q : 2 * Q]).astype(BF16)

        def project(target, left):
            @pl.loop(0, 4)
            def _(j):
                cols = pl.ds(pl.multiple_of(j * 512, 512), 512)
                from_cols = pl.ds(pl.multiple_of(left + j * 512, 512), 512)
                target[:, cols] = jnp.dot(
                    hidden[...], down[s, :, from_cols], preferred_element_type=F32
                ).astype(BF16)

        project(part_s.at[e, s], WIDTH)
        ring_s(e, s)[0]()
        project(part_t, 0)
        source, target, send_sem, recv_sem = in_t(e, s)
        pack_t(part_t, source)
        exchange(source, target, send_sem, recv_sem, 1)

    def finish_s(e, s):
        ring_s(e, s)[2]()

        @pl.loop(0, 4)
        def _(j):
            cols = pl.ds(pl.multiple_of(j * 512, 512), 512)
            part_s[e, s, 0:ROWS, cols] = (
                part_s[e, s, 0:ROWS, cols].astype(F32)
                + home_s[e, s, 0, :, cols].astype(F32)
                + home_s[e, s, 1, :, cols].astype(F32)
            ).astype(BF16)

        source, target, send_sem, recv_sem = in_s(e, s)
        pack_s(part_s.at[e, s], source)
        exchange(source, target, send_sem, recv_sem, 1)

    def collect_t(s):
        for e in range(2):
            source, target, send_sem, recv_sem = in_t(e, s)
            exchanged(source, target, send_sem, recv_sem).wait_recv()
            unpack_t(target, rows.at[1], e * WIDTH)
        for slot in (3, 1, 2, 0):
            first, second = to_tokens(key[slot][0], 0), to_tokens(key[slot][0], 1)
            at = slice(slot * ROWS, (slot + 1) * ROWS)
            target = block_t(s, slot, 0, 128)

            @pl.loop(0, 2)
            def _(j):
                cols = pl.ds(pl.multiple_of(j * 1024, 1024), 1024)
                cols_1 = pl.ds(pl.multiple_of(WIDTH + j * 1024, 1024), 1024)
                target[:, cols] = (
                    jnp.dot(first, rows[1, at, cols], preferred_element_type=F32)
                    + jnp.dot(second, rows[1, at, cols_1], preferred_element_type=F32)
                ).astype(BF16)

        ring_t(s)[0]()

    def result_copy(s, n):
        source = (down.at[s, 0:128, 0:WIDTH], down.at[s, 256:384, WIDTH:D])[n]
        target = (out_plus, out_minus)[s].at[:, n * WIDTH : (n + 1) * WIDTH]
        return pltpu.make_async_copy(source, target, o_sem.at[s, n])

    def result_s(s):
        for e in range(2):
            source, target, send_sem, recv_sem = in_s(e, s)
            exchanged(source, target, send_sem, recv_sem).wait_recv()
            unpack_s(target, rows.at[0], e * WIDTH)
        first, second = to_tokens(key[0][0], 0), to_tokens(key[0][0], 1)

        @pl.loop(0, 2)
        def _(j):
            cols = pl.ds(pl.multiple_of(j * 1024, 1024), 1024)
            cols_1 = pl.ds(pl.multiple_of(WIDTH + j * 1024, 1024), 1024)
            picked = jnp.dot(
                first, rows[0, 0:ROWS, cols], preferred_element_type=F32
            ) + jnp.dot(second, rows[0, 0:ROWS, cols_1], preferred_element_type=F32)
            down[s, 256:384, cols_1] = (probs * picked).astype(BF16)

        result_copy(s, 1).start()

    def result_t(s):
        ring_t(s)[2]()

        @pl.loop(0, 4)
        def _(j):
            cols = pl.ds(pl.multiple_of(j * 512, 512), 512)
            summed = (
                down[s, 0:128, cols].astype(F32)
                + home_t[s, 0, :, cols].astype(F32)
                + home_t[s, 1, :, cols].astype(F32)
            ).astype(BF16)
            down[s, 0:128, cols] = (probs * summed.astype(F32)).astype(BF16)

        result_copy(s, 0).start()

    probs = as_column(probs_row[...])
    loads[0].wait()
    loads[1].wait()
    move_wide(0, 0, 24)
    tokens_on()
    arrive_s(0)
    gather(0)
    move_wide(0, 24, 48)
    tokens_there()
    dispatch_t(0)
    dispatch_t(1)
    arrive_s(1)
    move_wide(0, 48, 72)
    pass_on(0)
    gather(1)
    move_wide(0, 72, 128)
    loads[2].wait()
    move_down(0, 0, 96)
    pass_on(1)
    gathered(0)
    arrive_t(0)
    multiply(0, 0)
    multiply(0, 1)
    loads = load_weights(1)
    for copy in loads:
        copy.start()
    arrive_t(1)

    @pl.loop(1, PEERS)
    def _(p):
        pl.semaphore_signal(free_sem, inc=1, device_id=(z, peer(p, -1)), device_id_type=MESH)

    loads[0].wait()
    loads[1].wait()
    move_wide(1, 0, 32)
    ring_s(0, 0)[1]()
    move_wide(1, 32, 96)
    ring_s(0, 1)[1]()
    move_wide(1, 96, 128)
    loads[2].wait()
    move_down(1, 0, 48)
    finish_s(0, 0)
    move_down(1, 48, 96)
    gathered(1)
    for e in range(2):
        exchanged(*out_t(e)).wait_send()
        exchanged(*out_s(e)).wait_send()
        for half in range(2):
            for copy in (gather_up(e, half), gather_down(e, half), gather_on(e, half)):
                copy.wait_send()
    pl.semaphore_wait(free_sem, PEERS - 1)
    multiply(1, 0)
    multiply(1, 1)
    finish_s(0, 1)
    ring_s(1, 0)[1]()
    ring_s(1, 1)[1]()
    collect_t(0)
    finish_s(1, 0)
    ring_t(0)[1]()
    finish_s(1, 1)
    collect_t(1)
    result_s(0)
    ring_t(1)[1]()
    result_t(0)
    result_s(1)
    result_t(1)

    for slot in (1, 2, 3):
        id_copy(slot).wait_send()
    for half in range(2):
        token_copy(True, half).wait_send()
        token_copy(False, half).wait_send()
        token_on(half).wait_send()
    for e in range(2):
        for s in range(2):
            ring_s(e, s)[3]()
            exchanged(*in_s(e, s)).wait_send()
            exchanged(*in_t(e, s)).wait_send()
    for s in range(2):
        ring_t(s)[3]()
        for n in range(2):
            result_copy(s, n).wait()


def shards(tokens, expert_ids, gate_probs, gate_weight, up_weight, down_weight, sign_offset):
    at = np.arange(768)
    swap = (at % 48 // 3 * 48 + at // 48 * 3 + at % 3).astype(np.int32).reshape(768, 1)
    slot = np.arange(ROWS)
    peer = slot // CAP
    slots = np.stack([peer // 8, peer // 2 % 4, peer % 2, slot % CAP], axis=1).astype(np.int32)
    vmem, hbm = pl.BlockSpec(memory_space=pltpu.VMEM), pl.BlockSpec(memory_space=pl.ANY)
    smem = pl.BlockSpec(memory_space=pltpu.SMEM)
    dma = pltpu.SemaphoreType.DMA
    return pl.pallas_call(
        kernel,
        out_shape=[jax.ShapeDtypeStruct((128, D), BF16)] * 2,
        in_specs=[vmem, vmem, smem, vmem, vmem, vmem, vmem, hbm, hbm, hbm],
        out_specs=[hbm, hbm],
        scratch_shapes=[
            pltpu.VMEM((4, 8, 128), I32),
            pltpu.VMEM((3, 128, WIDTH), BF16),
            pltpu.VMEM((2, 4 * ROWS, D), BF16),
            pltpu.VMEM((4, PEERS * MSG, 512), BF16),
            pltpu.VMEM((2, PEERS * MSG, 512), BF16),
            pltpu.VMEM((2, PEERS * MSG, 512), BF16),
            pltpu.VMEM((4, PEERS * MSG, 128), BF16),
            pltpu.VMEM((2, PEERS * MSG, 128), BF16),
            pltpu.VMEM((2, PEERS * MSG, 128), BF16),
            pltpu.VMEM((2, D, 2 * Q), BF16),
            pltpu.VMEM((2, Q, D), BF16),
            pltpu.VMEM((4 * ROWS, WIDTH), BF16),
            pltpu.VMEM((2, 2, 4 * ROWS, WIDTH), BF16),
            pltpu.VMEM((2, 2, ROWS, WIDTH), BF16),
            pltpu.VMEM((2, 2, 2, ROWS, WIDTH), BF16),
            pltpu.VMEM((2, 128, WIDTH), BF16),
            pltpu.VMEM((2, 2, 128, WIDTH), BF16),
            pltpu.VMEM((4 * ROWS, 2 * Q), F32),
            pltpu.VMEM((4 * ROWS, Q), BF16),
            pltpu.VMEM((768, 768), BF16),
            dma((3,)),
            dma((3,)),
            dma((3,)),
            dma((3, 2)),
            dma((3, 2)),
            dma((2,)),
            dma((2,)),
            dma((2,)),
            dma((2,)),
            dma((2, 6)),
            dma((2, 4, 2)),
            dma((2, 2, 6)),
            dma((2, 2, 2)),
            dma((2, 2, 2, 2)),
            dma((2, 6)),
            dma((2, 2)),
            dma((2, 2, 2)),
            dma((4,)),
            dma((4,)),
            dma((4,)),
            dma((4,)),
            dma((2, 2)),
            pltpu.SemaphoreType.REGULAR,
        ],
        compiler_params=pltpu.CompilerParams(
            collective_id=0, has_side_effects=True, vmem_limit_bytes=65_500_000
        ),
    )(
        expert_ids.reshape(1, 128),
        gate_probs.reshape(1, 128),
        sign_offset,
        jnp.asarray(swap),
        jnp.asarray(slots),
        jnp.asarray(slots.T),
        tokens,
        gate_weight,
        up_weight,
        down_weight,
    )


def solution(mesh):
    in_specs = (
        P(("dp", "mp"), None),
        P(("dp", "mp"), None),
        P(("dp", "mp"), None),
        P("mp", None, "dp"),
        P("mp", None, "dp"),
        P("mp", "dp", None),
        P(),
    )
    out_specs = (P(("dp", "mp"), None), P(("dp", "mp"), None))
    return jax.shard_map(shards, mesh=mesh, in_specs=in_specs, out_specs=out_specs, check_vma=False)
```

```python
import jax
import jax.numpy as jnp
import numpy as np
from jax import lax
from jax.experimental import pallas as pl
from jax.experimental.pallas import tpu as pltpu
from jax.sharding import PartitionSpec as P

D = 4096
FF = 1536
Q = 384
CAP = 3
ROWS = 96
HALF = 48
WIDTH = 2048
MSG = 48
PEERS = 32
EPS = 0.005
MESH = pl.DeviceIdType.MESH
F32, BF16, I32 = jnp.float32, jnp.bfloat16, jnp.int32


def mixing(number):
    number = number ^ lax.shift_right_logical(number, jnp.full_like(number, 16))
    number = number * 73244475
    number = number ^ lax.shift_right_logical(number, jnp.full_like(number, 16))
    number = number * 73244475
    return number ^ lax.shift_right_logical(number, jnp.full_like(number, 16))


def moved_by(position, offset_mixed):
    hashed = mixing(position ^ offset_mixed)
    return jnp.where((hashed & 512) != 0, EPS, -EPS).astype(F32)


def weigh(probs_row, plus, minus, out_plus, out_minus):
    same = lax.broadcasted_iota(I32, (128, 128), 0) == lax.broadcasted_iota(I32, (128, 128), 1)
    probs = jnp.sum(jnp.where(same, probs_row[...], 0.0), axis=1, keepdims=True)
    out_plus[...] = (probs * plus[...].astype(F32)).astype(BF16)
    out_minus[...] = (probs * minus[...].astype(F32)).astype(BF16)


def kernel(
    ids_row, sign_offset, swap, slots_col, slots_row, tokens, gate_w, up_w, down_w,
    out_plus, out_minus,
    ids_all, others, rows, sent_t, came_t, back_t, sent_s, came_s, back_s, wide, down, part_t, part_s,
    relay_s, home_s, relay_t, home_t, acc, hidden, perm,
    w_sem, i_send, i_recv, t_send, t_recv, xs_send, xs_recv, xt_send, xt_recv, z_send, z_recv,
    ps_send, rs_recv, hs_recv, pt_send, rt_recv, ht_recv, bs_send, bs_recv, bt_send, bt_recv, o_sem,
    free_sem,
):
    z, m = lax.axis_index("dp"), lax.axis_index("mp")
    x, y, core = lax.div(m, 8), lax.rem(lax.div(m, 2), 4), lax.rem(m, 2)
    above, below, across = (z + 1) % 4, (z + 3) % 4, (z + 2) % 4
    hidden_base = z * Q

    def peer(p, sign):
        a, b = lax.div(p, 8), lax.rem(lax.div(p, 2), 4)
        return (
            lax.rem(x + sign * a + 4, 4) * 8
            + lax.rem(y + sign * b + 4, 4) * 2
            + lax.rem(core + p, 2)
        )

    def remote(source, target, send_sem, recv_sem, device):
        return pltpu.make_async_remote_copy(
            source, target, send_sem, recv_sem, device_id=device, device_id_type=MESH
        )

    def load_weights(e):
        return [
            pltpu.make_async_copy(source.at[e], target, w_sem.at[i])
            for i, (source, target) in enumerate(
                (
                    (gate_w, wide.at[0, :, 0:Q]),
                    (up_w, wide.at[0, :, Q : 2 * Q]),
                    (down_w, down.at[0]),
                )
            )
        ]

    loads = load_weights(0)
    for copy in loads:
        copy.start()

    barrier = pltpu.get_barrier_semaphore()

    @pl.loop(1, PEERS)
    def _(p):
        pl.semaphore_signal(barrier, inc=1, device_id=(z, peer(p, -1)), device_id_type=MESH)

    for near in (above, below, across):
        pl.semaphore_signal(barrier, inc=1, device_id=(near, m), device_id_type=MESH)
    ids_all[0] = jnp.broadcast_to(ids_row[...], (8, 128))
    pl.semaphore_wait(barrier, PEERS + 2)

    def token_copy(up, half):
        at = slice(half * 64, half * 64 + 64)
        return remote(
            tokens.at[at, 0:WIDTH], others.at[0 if up else 1, at], t_send.at[0 if up else 1, half],
            t_recv.at[0 if up else 1, half], (above if up else below, m),
        )

    def token_on(half):
        at = slice(half * 64, half * 64 + 64)
        return remote(
            others.at[half, at], others.at[2, at], t_send.at[2, half], t_recv.at[2, half],
            ((above, below)[half], m),
        )

    def id_copy(slot):
        device = (above, below, across)[slot - 1]
        return remote(
            ids_all.at[0], ids_all.at[slot], i_send.at[slot - 1], i_recv.at[slot - 1], (device, m)
        )

    for slot in (1, 2, 3):
        id_copy(slot).start()
    for half in range(2):
        token_copy(True, half).start()
        token_copy(False, 1 - half).start()

    at_row = lax.broadcasted_iota(I32, (128, 128), 0)
    at_col = lax.broadcasted_iota(I32, (128, 128), 1)

    def as_column(row):
        return jnp.sum(jnp.where(at_row == at_col, row, jnp.zeros_like(row)), axis=1, keepdims=True)

    def keys(slot):
        row = ids_all[slot][0:1]
        column = as_column(row)
        alike = column == row
        key_col = column * 4 + jnp.sum(
            jnp.where(alike & (at_col < at_row), 1, 0), axis=1, keepdims=True
        )
        key_row = row * 4 + jnp.sum(
            jnp.where(alike & (at_row < at_col), 1, 0), axis=0, keepdims=True
        )
        return key_col, key_row

    def slot_keys(a, b, d, s, e):
        owner = ((x - a) & 3) * 8 + ((y - b) & 3) * 2 + ((core + d) & 1)
        return (owner * 2 + e) * 4 + s

    def one_hot(found):
        return jnp.where(found, 1.0, 0.0).astype(BF16)

    def to_slots(key_row, e):
        return one_hot(key_row == slot_keys(*[slots_col[:, i : i + 1] for i in range(4)], e))

    def to_tokens(key_col, e):
        return one_hot(key_col == slot_keys(*[slots_row[i : i + 1, :] for i in range(4)], e))

    perm[...] = one_hot(lax.broadcasted_iota(I32, (768, 768), 1) == swap[...])

    def swapped(value):
        return jnp.dot(perm[...], value, preferred_element_type=F32).astype(BF16)

    def pack(source, first, target):
        laid = swapped(
            jnp.concatenate(
                [
                    jnp.concatenate(
                        [
                            source[
                                first + half * HALF : first + (half + 1) * HALF,
                                c * 128 : (c + 1) * 128,
                            ]
                            for half in range(2)
                        ],
                        axis=1,
                    )
                    for c in range(16)
                ],
                axis=0,
            )
        )
        for half in range(2):
            target[half * 768 : (half + 1) * 768, :] = laid[:, half * 128 : (half + 1) * 128]

    def unpack(source, target, first, left):
        laid = swapped(jnp.concatenate([source[0:768, :], source[768:1536, :]], axis=1))
        for half in range(2):
            for c in range(16):
                target[
                    first + half * HALF : first + (half + 1) * HALF,
                    left + c * 128 : left + (c + 1) * 128,
                ] = laid[c * HALF : (c + 1) * HALF, half * 128 : (half + 1) * 128]

    def exchange(source, target, send_sem, recv_sem, sign):
        @pl.loop(1, PEERS)
        def _(p):
            at = pl.ds(pl.multiple_of(p * MSG, MSG), MSG)
            remote(
                source.at[at], target.at[at], send_sem, recv_sem, (z, peer(p, sign))
            ).start()

        target[0:MSG, :] = source[0:MSG, :]

    def exchanged(source, target, send_sem, recv_sem):
        return remote(
            source.at[MSG : PEERS * MSG], target.at[MSG : PEERS * MSG], send_sem, recv_sem,
            (z, peer(jnp.int32(1), 1)),
        )

    def out_s(e):
        return sent_s.at[e], came_s.at[e], xs_send.at[e], xs_recv.at[e]

    def out_t(e, slot):
        return sent_t.at[e, slot], came_t.at[e, slot], xt_send.at[e, slot], xt_recv.at[e, slot]

    def in_s(e, s):
        i = 2 * e + s
        if e == 0:
            return sent_s.at[2 + s], back_s.at[s], bs_send.at[i], bs_recv.at[i]
        return sent_s.at[s], came_s.at[s], bs_send.at[i], bs_recv.at[i]

    def in_t(e, s, slot):
        i = 2 * e + s
        if e == 0:
            return sent_t.at[2 + s, slot], back_t.at[s, slot], bt_send.at[i, slot], bt_recv.at[i, slot]
        return sent_t.at[s, slot], came_t.at[s, slot], bt_send.at[i, slot], bt_recv.at[i, slot]

    key = {0: keys(0)}

    def select(e, slot, value, target, first):
        chosen = to_slots(key[slot][1], e)
        for c in range(2):
            target[first : first + ROWS, c * 1024 : (c + 1) * 1024] = jnp.dot(
                chosen, value(slice(c * 1024, (c + 1) * 1024)), preferred_element_type=F32
            ).astype(BF16)

    def dispatch_s(e):
        staged = part_s.at[0, e]
        select(e, 0, lambda cols: tokens[:, WIDTH + cols.start : WIDTH + cols.stop], staged, 0)
        pack(staged, 0, sent_s.at[e])
        exchange(*out_s(e), -1)

    def dispatch_t(e, slot):
        value = (lambda cols: tokens[:, cols]) if slot == 0 else (lambda cols: others[slot - 1, :, cols])
        select(e, slot, value, part_t, slot * ROWS)
        pack(part_t, slot * ROWS, sent_t.at[e, slot])
        exchange(*out_t(e, slot), -1)

    offset_mixed = mixing(sign_offset[0] * 668265261 + 12345)

    def move_wide(e, lo, hi):
        expert = m * 2 + e
        inner = lax.broadcasted_iota(I32, (32, Q), 0) * (3 * FF) + lax.broadcasted_iota(
            I32, (32, Q), 1
        ) * 3

        @pl.loop(lo, hi)
        def _(i):
            at = pl.ds(pl.multiple_of(i * 32, 32), 32)
            first = ((expert * D + i * 32) * FF + hidden_base) * 3
            for tag in range(2):
                cols = slice(tag * Q, (tag + 1) * Q)
                weight = wide[0, at, cols].astype(F32)
                step = moved_by(inner + (first + tag), offset_mixed)
                wide[0, at, cols] = (weight + step).astype(BF16)
                wide[1, at, cols] = (weight - step).astype(BF16)

    def move_down(e, lo, hi):
        expert = m * 2 + e
        inner = lax.broadcasted_iota(I32, (32, 512), 0) * (3 * D) + lax.broadcasted_iota(
            I32, (32, 512), 1
        ) * 3

        @pl.loop(lo, hi)
        def _(i):
            row, col = i // 8 * 32, i % 8 * 512
            at, cols = pl.ds(pl.multiple_of(row, 32), 32), pl.ds(pl.multiple_of(col, 512), 512)
            first = ((expert * FF + hidden_base + row) * D + col) * 3 + 2
            weight = down[0, at, cols].astype(F32)
            step = moved_by(inner + first, offset_mixed)
            down[0, at, cols] = (weight + step).astype(BF16)
            down[1, at, cols] = (weight - step).astype(BF16)

    def tokens_on():
        token_copy(True, 0).wait_recv()
        token_on(0).start()
        token_copy(False, 1).wait_recv()
        token_on(1).start()

    def tokens_there(slot):
        if slot == 3:
            for half in range(2):
                token_on(half).wait_recv()
        else:
            token_copy(slot == 1, 2 - slot).wait_recv()
        id_copy(slot).wait_recv()
        key[slot] = keys(slot)

    def arrive_t(e, slot):
        exchanged(*out_t(e, slot)).wait_recv()
        unpack(came_t.at[e, slot], rows.at[e], slot * ROWS, 0)

    def arrive_s(e):
        exchanged(*out_s(e)).wait_recv()
        unpack(came_s.at[e], rows.at[e], 0, WIDTH)

    def gather_copy(e, from_slot, to_slot, half, n, to):
        a, b = from_slot * ROWS + half * HALF, to_slot * ROWS + half * HALF
        return remote(
            rows.at[e, a : a + HALF, WIDTH:D], rows.at[e, b : b + HALF, WIDTH:D],
            z_send.at[e, n], z_recv.at[e, to_slot, half], (to, m),
        )

    def gather_up(e, half):
        return gather_copy(e, 0, 1, half, half, above)

    def gather_down(e, half):
        return gather_copy(e, 0, 2, half, 2 + half, below)

    def gather_on(e, half):
        return gather_copy(e, 1 + half, 3, half, 4 + half, (above, below)[half])

    def gather(e):
        for half in range(2):
            gather_up(e, half).start()
            gather_down(e, 1 - half).start()

    def pass_on(e):
        gather_up(e, 0).wait_recv()
        gather_on(e, 0).start()
        gather_down(e, 1).wait_recv()
        gather_on(e, 1).start()

    def gathered(e):
        gather_up(e, 1).wait_recv()
        gather_down(e, 0).wait_recv()
        for half in range(2):
            gather_on(e, half).wait_recv()

    def ring(block, relay, home, send_sem, relay_sem, home_sem):
        def copy(which):
            if which < 2:
                half = which
                return remote(
                    block(3, half), relay(half), send_sem.at[which], relay_sem.at[half],
                    ((below, above)[half], m),
                )
            k, half = ((0, 1), (1, 0), (0, 0), (1, 1))[which - 2]
            return remote(
                block(1 + k, half), home(k, half), send_sem.at[which], home_sem.at[k, half],
                ((below, above)[k], m),
            )

        def start(*which):
            for n in which:
                copy(n).start()

        def pass_sum():
            for k in range(2):
                copy(k).wait_recv()
                mine, arrived = block(1 + k, k), relay(k)

                @pl.loop(0, 4)
                def _(j):
                    cols = pl.ds(pl.multiple_of(j * 512, 512), 512)
                    mine[:, cols] = (
                        mine[:, cols].astype(F32) + arrived[:, cols].astype(F32)
                    ).astype(BF16)

                copy(4 + k).start()

        def wait_home():
            for which in range(2, 6):
                copy(which).wait_recv()

        def wait_sent():
            for which in range(6):
                copy(which).wait_send()

        return start, pass_sum, wait_home, wait_sent

    def ring_s(e, s):
        def block(slot, half):
            return part_s.at[e, s, slot * ROWS + half * HALF : slot * ROWS + (half + 1) * HALF]

        return ring(
            block,
            lambda half: relay_s.at[e, s, half * HALF : (half + 1) * HALF],
            lambda k, half: home_s.at[e, s, k, half * HALF : (half + 1) * HALF],
            ps_send.at[e, s], rs_recv.at[e, s], hs_recv.at[e, s],
        )

    def block_t(s, slot, lo, hi):
        top, left = slot // 2 * 128, slot % 2 * WIDTH
        return down.at[s, top + lo : top + hi, left : left + WIDTH]

    def ring_t(s):
        return ring(
            lambda slot, half: block_t(s, slot, half * 64, half * 64 + 64),
            lambda half: relay_t.at[s, half * 64 : half * 64 + 64],
            lambda k, half: home_t.at[s, k, half * 64 : half * 64 + 64],
            pt_send.at[s], rt_recv.at[s], ht_recv.at[s],
        )

    def multiply(e, s):
        acc[...] = jnp.zeros_like(acc)

        @pl.loop(0, 8)
        def _(k):
            at = pl.ds(pl.multiple_of(k * 512, 512), 512)
            acc[...] += jnp.dot(rows[e, :, at], wide[s, at, :], preferred_element_type=F32)

        @pl.loop(0, 8)
        def _(i):
            at = pl.ds(pl.multiple_of(i * HALF, HALF), HALF)
            gate = acc[at, 0:Q]
            hidden[at, :] = (gate / (1.0 + jnp.exp(-gate)) * acc[at, Q : 2 * Q]).astype(BF16)

        def project(target, left):
            @pl.loop(0, 4)
            def _(j):
                cols = pl.ds(pl.multiple_of(j * 512, 512), 512)
                from_cols = pl.ds(pl.multiple_of(left + j * 512, 512), 512)
                target[:, cols] = jnp.dot(
                    hidden[...], down[s, :, from_cols], preferred_element_type=F32
                ).astype(BF16)

        project(part_s.at[e, s], WIDTH)
        ring_s(e, s)[0](0, 1, 2, 3)
        project(part_t, 0)
        for slot in (3, 1, 2, 0):
            pack(part_t, slot * ROWS, in_t(e, s, slot)[0])
            exchange(*in_t(e, s, slot), 1)

    def finish_s(e, s):
        ring_s(e, s)[2]()

        @pl.loop(0, 4)
        def _(j):
            cols = pl.ds(pl.multiple_of(j * 512, 512), 512)
            part_s[e, s, 0:ROWS, cols] = (
                part_s[e, s, 0:ROWS, cols].astype(F32)
                + home_s[e, s, 0, :, cols].astype(F32)
                + home_s[e, s, 1, :, cols].astype(F32)
            ).astype(BF16)

        pack(part_s.at[e, s], 0, in_s(e, s)[0])
        exchange(*in_s(e, s), 1)

    def collect_t(s):
        for slot in (3, 1, 2, 0):
            for e in range(2):
                exchanged(*in_t(e, s, slot)).wait_recv()
                unpack(in_t(e, s, slot)[1], rows.at[1], slot * ROWS, e * WIDTH)
            first, second = to_tokens(key[slot][0], 0), to_tokens(key[slot][0], 1)
            at = slice(slot * ROWS, (slot + 1) * ROWS)
            for j in range(2):
                cols = slice(j * 1024, (j + 1) * 1024)
                cols_1 = slice(WIDTH + j * 1024, WIDTH + (j + 1) * 1024)
                block_t(s, slot, 0, 128)[:, cols] = (
                    jnp.dot(first, rows[1, at, cols], preferred_element_type=F32)
                    + jnp.dot(second, rows[1, at, cols_1], preferred_element_type=F32)
                ).astype(BF16)
            ring_t(s)[0](*{3: (0, 1), 1: (2,), 2: (3,), 0: ()}[slot])

    def result_copy(s, n):
        source = (down.at[s, 0:128, 0:WIDTH], down.at[s, 256:384, WIDTH:D])[n]
        target = (out_plus, out_minus)[s].at[:, n * WIDTH : (n + 1) * WIDTH]
        return pltpu.make_async_copy(source, target, o_sem.at[s, n])

    def result_s(s):
        for e in range(2):
            exchanged(*in_s(e, s)).wait_recv()
            unpack(in_s(e, s)[1], rows.at[0], 0, e * WIDTH)
        first, second = to_tokens(key[0][0], 0), to_tokens(key[0][0], 1)

        @pl.loop(0, 2)
        def _(j):
            cols = pl.ds(pl.multiple_of(j * 1024, 1024), 1024)
            cols_1 = pl.ds(pl.multiple_of(WIDTH + j * 1024, 1024), 1024)
            picked = jnp.dot(
                first, rows[0, 0:ROWS, cols], preferred_element_type=F32
            ) + jnp.dot(second, rows[0, 0:ROWS, cols_1], preferred_element_type=F32)
            down[s, 256:384, cols_1] = picked.astype(BF16)

        result_copy(s, 1).start()

    def result_t(s):
        ring_t(s)[2]()

        @pl.loop(0, 4)
        def _(j):
            cols = pl.ds(pl.multiple_of(j * 512, 512), 512)
            down[s, 0:128, cols] = (
                down[s, 0:128, cols].astype(F32)
                + home_t[s, 0, :, cols].astype(F32)
                + home_t[s, 1, :, cols].astype(F32)
            ).astype(BF16)

        result_copy(s, 0).start()

    dispatch_t(0, 0)
    dispatch_s(0)
    dispatch_t(1, 0)
    loads[0].wait()
    loads[1].wait()
    move_wide(0, 0, 24)
    tokens_on()
    move_wide(0, 24, 56)
    for slot in (1, 2):
        tokens_there(slot)
        dispatch_t(0, slot)
    arrive_s(0)
    gather(0)
    move_wide(0, 56, 88)
    tokens_there(3)
    dispatch_t(0, 3)
    dispatch_s(1)
    for slot in (1, 2, 3):
        dispatch_t(1, slot)
    move_wide(0, 88, 128)
    pass_on(0)
    loads[2].wait()
    move_down(0, 0, 48)
    arrive_t(0, 0)
    arrive_s(1)
    gather(1)
    move_down(0, 48, 96)
    for slot in (1, 2, 3):
        arrive_t(0, slot)
    gathered(0)
    multiply(0, 0)
    pass_on(1)
    multiply(0, 1)
    loads = load_weights(1)
    for copy in loads:
        copy.start()
    for slot in range(4):
        arrive_t(1, slot)

    @pl.loop(1, PEERS)
    def _(p):
        pl.semaphore_signal(free_sem, inc=1, device_id=(z, peer(p, -1)), device_id_type=MESH)

    loads[0].wait()
    loads[1].wait()
    move_wide(1, 0, 32)
    ring_s(0, 0)[1]()
    move_wide(1, 32, 96)
    ring_s(0, 1)[1]()
    move_wide(1, 96, 128)
    loads[2].wait()
    move_down(1, 0, 48)
    finish_s(0, 0)
    move_down(1, 48, 96)
    gathered(1)
    for e in range(2):
        for slot in range(4):
            exchanged(*out_t(e, slot)).wait_send()
        exchanged(*out_s(e)).wait_send()
        for half in range(2):
            for copy in (gather_up(e, half), gather_down(e, half), gather_on(e, half)):
                copy.wait_send()
    pl.semaphore_wait(free_sem, PEERS - 1)
    multiply(1, 0)
    multiply(1, 1)
    finish_s(0, 1)
    ring_s(1, 0)[1]()
    ring_s(1, 1)[1]()
    collect_t(0)
    finish_s(1, 0)
    ring_t(0)[1]()
    finish_s(1, 1)
    collect_t(1)
    result_s(0)
    ring_t(1)[1]()
    result_t(0)
    result_s(1)
    result_t(1)

    for slot in (1, 2, 3):
        id_copy(slot).wait_send()
    for half in range(2):
        token_copy(True, half).wait_send()
        token_copy(False, half).wait_send()
        token_on(half).wait_send()
    for e in range(2):
        for s in range(2):
            ring_s(e, s)[3]()
            exchanged(*in_s(e, s)).wait_send()
            for slot in range(4):
                exchanged(*in_t(e, s, slot)).wait_send()
    for s in range(2):
        ring_t(s)[3]()
        for n in range(2):
            result_copy(s, n).wait()


def shards(tokens, expert_ids, gate_probs, gate_weight, up_weight, down_weight, sign_offset):
    at = np.arange(768)
    swap = (at % 48 // 3 * 48 + at // 48 * 3 + at % 3).astype(np.int32).reshape(768, 1)
    slot = np.arange(ROWS)
    peer = slot // CAP
    slots = np.stack([peer // 8, peer // 2 % 4, peer % 2, slot % CAP], axis=1).astype(np.int32)
    vmem, hbm = pl.BlockSpec(memory_space=pltpu.VMEM), pl.BlockSpec(memory_space=pl.ANY)
    smem = pl.BlockSpec(memory_space=pltpu.SMEM)
    dma = pltpu.SemaphoreType.DMA
    plus, minus = pl.pallas_call(
        kernel,
        out_shape=[jax.ShapeDtypeStruct((128, D), BF16)] * 2,
        in_specs=[vmem, smem, vmem, vmem, vmem, vmem, hbm, hbm, hbm],
        out_specs=[hbm, hbm],
        scratch_shapes=[
            pltpu.VMEM((4, 8, 128), I32),
            pltpu.VMEM((3, 128, WIDTH), BF16),
            pltpu.VMEM((2, 4 * ROWS, D), BF16),
            pltpu.VMEM((4, 4, PEERS * MSG, 128), BF16),
            pltpu.VMEM((2, 4, PEERS * MSG, 128), BF16),
            pltpu.VMEM((2, 4, PEERS * MSG, 128), BF16),
            pltpu.VMEM((4, PEERS * MSG, 128), BF16),
            pltpu.VMEM((2, PEERS * MSG, 128), BF16),
            pltpu.VMEM((2, PEERS * MSG, 128), BF16),
            pltpu.VMEM((2, D, 2 * Q), BF16),
            pltpu.VMEM((2, Q, D), BF16),
            pltpu.VMEM((4 * ROWS, WIDTH), BF16),
            pltpu.VMEM((2, 2, 4 * ROWS, WIDTH), BF16),
            pltpu.VMEM((2, 2, ROWS, WIDTH), BF16),
            pltpu.VMEM((2, 2, 2, ROWS, WIDTH), BF16),
            pltpu.VMEM((2, 128, WIDTH), BF16),
            pltpu.VMEM((2, 2, 128, WIDTH), BF16),
            pltpu.VMEM((4 * ROWS, 2 * Q), F32),
            pltpu.VMEM((4 * ROWS, Q), BF16),
            pltpu.VMEM((768, 768), BF16),
            dma((3,)),
            dma((3,)),
            dma((3,)),
            dma((3, 2)),
            dma((3, 2)),
            dma((2,)),
            dma((2,)),
            dma((2, 4)),
            dma((2, 4)),
            dma((2, 6)),
            dma((2, 4, 2)),
            dma((2, 2, 6)),
            dma((2, 2, 2)),
            dma((2, 2, 2, 2)),
            dma((2, 6)),
            dma((2, 2)),
            dma((2, 2, 2)),
            dma((4,)),
            dma((4,)),
            dma((4, 4)),
            dma((4, 4)),
            dma((2, 2)),
            pltpu.SemaphoreType.REGULAR,
        ],
        compiler_params=pltpu.CompilerParams(
            collective_id=0, has_side_effects=True, vmem_limit_bytes=65_500_000
        ),
    )(
        expert_ids.reshape(1, 128),
        sign_offset,
        jnp.asarray(swap),
        jnp.asarray(slots),
        jnp.asarray(slots.T),
        tokens,
        gate_weight,
        up_weight,
        down_weight,
    )
    block = pl.BlockSpec((128, 1024), lambda i: (0, i))
    return pl.pallas_call(
        weigh,
        out_shape=[jax.ShapeDtypeStruct((128, D), BF16)] * 2,
        grid=(4,),
        in_specs=[pl.BlockSpec((1, 128), lambda i: (0, 0)), block, block],
        out_specs=[block, block],
    )(gate_probs.reshape(1, 128), plus, minus)


def solution(mesh):
    in_specs = (
        P(("dp", "mp"), None),
        P(("dp", "mp"), None),
        P(("dp", "mp"), None),
        P("mp", None, "dp"),
        P("mp", None, "dp"),
        P("mp", "dp", None),
        P(),
    )
    out_specs = (P(("dp", "mp"), None), P(("dp", "mp"), None))
    return jax.shard_map(shards, mesh=mesh, in_specs=in_specs, out_specs=out_specs, check_vma=False)
```

```python
import jax
import jax.numpy as jnp
import numpy as np
from jax import lax
from jax.experimental import pallas as pl
from jax.experimental.pallas import tpu as pltpu
from jax.sharding import PartitionSpec as P

D = 4096
FF = 1536
Q = 384
CAP = 3
ROWS = 96
HALF = 48
WIDTH = 2048
MSG = 48
PEERS = 32
EPS = 0.005
MESH = pl.DeviceIdType.MESH
F32, BF16, I32 = jnp.float32, jnp.bfloat16, jnp.int32


def mixing(number):
    number = number ^ lax.shift_right_logical(number, jnp.full_like(number, 16))
    number = number * 73244475
    number = number ^ lax.shift_right_logical(number, jnp.full_like(number, 16))
    number = number * 73244475
    return number ^ lax.shift_right_logical(number, jnp.full_like(number, 16))


def moved_by(position, offset_mixed):
    hashed = mixing(position ^ offset_mixed)
    return jnp.where((hashed & 512) != 0, EPS, -EPS).astype(F32)


def weigh(probs_row, plus, minus, out_plus, out_minus):
    same = lax.broadcasted_iota(I32, (128, 128), 0) == lax.broadcasted_iota(I32, (128, 128), 1)
    probs = jnp.sum(jnp.where(same, probs_row[...], 0.0), axis=1, keepdims=True)
    out_plus[...] = (probs * plus[...].astype(F32)).astype(BF16)
    out_minus[...] = (probs * minus[...].astype(F32)).astype(BF16)


def kernel(
    ids_row, sign_offset, swap, slots_col, slots_row, tokens, gate_w, up_w, down_w,
    out_plus, out_minus,
    ids_all, others, rows, sent_t, came_t, back_t, sent_s, came_s, back_s, wide, down, part_t, part_s,
    relay_s, home_s, relay_t, home_t, acc, hidden, perm,
    w_sem, i_send, i_recv, t_send, t_recv, xs_send, xs_recv, xt_send, xt_recv, z_send, z_recv,
    ps_send, rs_recv, hs_recv, pt_send, rt_recv, ht_recv, bs_send, bs_recv, bt_send, bt_recv, o_sem,
    free_sem,
):
    z, m = lax.axis_index("dp"), lax.axis_index("mp")
    x, y, core = lax.div(m, 8), lax.rem(lax.div(m, 2), 4), lax.rem(m, 2)
    above, below, across = (z + 1) % 4, (z + 3) % 4, (z + 2) % 4
    hidden_base = z * Q

    def peer(p, sign):
        a, b = lax.div(p, 8), lax.rem(lax.div(p, 2), 4)
        return (
            lax.rem(x + sign * a + 4, 4) * 8
            + lax.rem(y + sign * b + 4, 4) * 2
            + lax.rem(core + p, 2)
        )

    def remote(source, target, send_sem, recv_sem, device):
        return pltpu.make_async_remote_copy(
            source, target, send_sem, recv_sem, device_id=device, device_id_type=MESH
        )

    def load_weights(e):
        return [
            pltpu.make_async_copy(source.at[e], target, w_sem.at[i])
            for i, (source, target) in enumerate(
                (
                    (gate_w, wide.at[0, :, 0:Q]),
                    (up_w, wide.at[0, :, Q : 2 * Q]),
                    (down_w, down.at[0]),
                )
            )
        ]

    loads = load_weights(0)
    for copy in loads:
        copy.start()

    barrier = pltpu.get_barrier_semaphore()

    @pl.loop(1, PEERS)
    def _(p):
        pl.semaphore_signal(barrier, inc=1, device_id=(z, peer(p, -1)), device_id_type=MESH)

    for near in (above, below, across):
        pl.semaphore_signal(barrier, inc=1, device_id=(near, m), device_id_type=MESH)
    ids_all[0] = jnp.broadcast_to(ids_row[...], (8, 128))
    pl.semaphore_wait(barrier, PEERS + 2)

    def token_copy(up, half):
        at = slice(half * 64, half * 64 + 64)
        return remote(
            tokens.at[at, 0:WIDTH], others.at[0 if up else 1, at], t_send.at[0 if up else 1, half],
            t_recv.at[0 if up else 1, half], (above if up else below, m),
        )

    def token_on(half):
        at = slice(half * 64, half * 64 + 64)
        return remote(
            others.at[half, at], others.at[2, at], t_send.at[2, half], t_recv.at[2, half],
            ((above, below)[half], m),
        )

    def id_copy(slot):
        device = (above, below, across)[slot - 1]
        return remote(
            ids_all.at[0], ids_all.at[slot], i_send.at[slot - 1], i_recv.at[slot - 1], (device, m)
        )

    for slot in (1, 2, 3):
        id_copy(slot).start()
    for half in range(2):
        token_copy(True, half).start()
        token_copy(False, 1 - half).start()

    at_row = lax.broadcasted_iota(I32, (128, 128), 0)
    at_col = lax.broadcasted_iota(I32, (128, 128), 1)

    def as_column(row):
        return jnp.sum(jnp.where(at_row == at_col, row, jnp.zeros_like(row)), axis=1, keepdims=True)

    def keys(slot):
        row = ids_all[slot][0:1]
        column = as_column(row)
        alike = column == row
        key_col = column * 4 + jnp.sum(
            jnp.where(alike & (at_col < at_row), 1, 0), axis=1, keepdims=True
        )
        key_row = row * 4 + jnp.sum(
            jnp.where(alike & (at_row < at_col), 1, 0), axis=0, keepdims=True
        )
        return key_col, key_row

    def slot_keys(a, b, d, s, e):
        owner = ((x - a) & 3) * 8 + ((y - b) & 3) * 2 + ((core + d) & 1)
        return (owner * 2 + e) * 4 + s

    def one_hot(found):
        return jnp.where(found, 1.0, 0.0).astype(BF16)

    def to_slots(key_row, e):
        return one_hot(key_row == slot_keys(*[slots_col[:, i : i + 1] for i in range(4)], e))

    def to_tokens(key_col, e):
        return one_hot(key_col == slot_keys(*[slots_row[i : i + 1, :] for i in range(4)], e))

    perm[...] = one_hot(lax.broadcasted_iota(I32, (256, 256), 1) == swap[...])

    def swapped(value):
        return jnp.dot(perm[...], value, preferred_element_type=F32).astype(BF16)

    def pack(source, first, target):
        laid = swapped(
            jnp.concatenate(
                [
                    jnp.concatenate(
                        [
                            source[first + k * 16 : first + (k + 1) * 16, c * 128 : (c + 1) * 128]
                            for k in range(2 * CAP)
                        ],
                        axis=1,
                    )
                    for c in range(16)
                ],
                axis=0,
            )
        )
        for k in range(2 * CAP):
            for p in range(16):
                to = (k % 2 * 16 + p) * MSG + k // 2 * 16
                target[to : to + 16, :] = laid[p * 16 : (p + 1) * 16, k * 128 : (k + 1) * 128]

    def unpack(source, target, first, left):
        laid = swapped(
            jnp.concatenate(
                [
                    jnp.concatenate(
                        [
                            source[
                                (k % 2 * 16 + p) * MSG + k // 2 * 16 : (k % 2 * 16 + p) * MSG
                                + (k // 2 + 1) * 16,
                                :,
                            ]
                            for k in range(2 * CAP)
                        ],
                        axis=1,
                    )
                    for p in range(16)
                ],
                axis=0,
            )
        )
        for k in range(2 * CAP):
            for c in range(16):
                target[
                    first + k * 16 : first + (k + 1) * 16, left + c * 128 : left + (c + 1) * 128
                ] = laid[c * 16 : (c + 1) * 16, k * 128 : (k + 1) * 128]

    def exchange(source, target, send_sem, recv_sem, sign):
        @pl.loop(1, PEERS)
        def _(p):
            at = pl.ds(pl.multiple_of(p * MSG, MSG), MSG)
            remote(
                source.at[at], target.at[at], send_sem, recv_sem, (z, peer(p, sign))
            ).start()

        target[0:MSG, :] = source[0:MSG, :]

    def exchanged(source, target, send_sem, recv_sem):
        return remote(
            source.at[MSG : PEERS * MSG], target.at[MSG : PEERS * MSG], send_sem, recv_sem,
            (z, peer(jnp.int32(1), 1)),
        )

    def out_s(e):
        return sent_s.at[e], came_s.at[e], xs_send.at[e], xs_recv.at[e]

    def out_t(e, slot):
        return sent_t.at[e, slot], came_t.at[e, slot], xt_send.at[e, slot], xt_recv.at[e, slot]

    def in_s(e, s):
        i = 2 * e + s
        if e == 0:
            return sent_s.at[2 + s], back_s.at[s], bs_send.at[i], bs_recv.at[i]
        return sent_s.at[s], came_s.at[s], bs_send.at[i], bs_recv.at[i]

    def in_t(e, s, slot):
        i = 2 * e + s
        if e == 0:
            return sent_t.at[2 + s, slot], back_t.at[s, slot], bt_send.at[i, slot], bt_recv.at[i, slot]
        return sent_t.at[s, slot], came_t.at[s, slot], bt_send.at[i, slot], bt_recv.at[i, slot]

    key = {0: keys(0)}

    def select(e, slot, value, target, first):
        chosen = to_slots(key[slot][1], e)
        for c in range(2):
            target[first : first + ROWS, c * 1024 : (c + 1) * 1024] = jnp.dot(
                chosen, value(slice(c * 1024, (c + 1) * 1024)), preferred_element_type=F32
            ).astype(BF16)

    def dispatch_s(e):
        staged = part_s.at[0, e]
        select(e, 0, lambda cols: tokens[:, WIDTH + cols.start : WIDTH + cols.stop], staged, 0)
        pack(staged, 0, sent_s.at[e])
        exchange(*out_s(e), -1)

    def dispatch_t(e, slot):
        value = (lambda cols: tokens[:, cols]) if slot == 0 else (lambda cols: others[slot - 1, :, cols])
        select(e, slot, value, part_t, slot * ROWS)
        pack(part_t, slot * ROWS, sent_t.at[e, slot])
        exchange(*out_t(e, slot), -1)

    offset_mixed = mixing(sign_offset[0] * 668265261 + 12345)

    def move_wide(e, lo, hi):
        expert = m * 2 + e
        inner = lax.broadcasted_iota(I32, (32, Q), 0) * (3 * FF) + lax.broadcasted_iota(
            I32, (32, Q), 1
        ) * 3

        @pl.loop(lo, hi)
        def _(i):
            at = pl.ds(pl.multiple_of(i * 32, 32), 32)
            first = ((expert * D + i * 32) * FF + hidden_base) * 3
            for tag in range(2):
                cols = slice(tag * Q, (tag + 1) * Q)
                weight = wide[0, at, cols].astype(F32)
                step = moved_by(inner + (first + tag), offset_mixed)
                wide[0, at, cols] = (weight + step).astype(BF16)
                wide[1, at, cols] = (weight - step).astype(BF16)

    def move_down(e, lo, hi):
        expert = m * 2 + e
        inner = lax.broadcasted_iota(I32, (32, 512), 0) * (3 * D) + lax.broadcasted_iota(
            I32, (32, 512), 1
        ) * 3

        @pl.loop(lo, hi)
        def _(i):
            row, col = i // 8 * 32, i % 8 * 512
            at, cols = pl.ds(pl.multiple_of(row, 32), 32), pl.ds(pl.multiple_of(col, 512), 512)
            first = ((expert * FF + hidden_base + row) * D + col) * 3 + 2
            weight = down[0, at, cols].astype(F32)
            step = moved_by(inner + first, offset_mixed)
            down[0, at, cols] = (weight + step).astype(BF16)
            down[1, at, cols] = (weight - step).astype(BF16)

    def tokens_on():
        token_copy(True, 0).wait_recv()
        token_on(0).start()
        token_copy(False, 1).wait_recv()
        token_on(1).start()

    def tokens_there(slot):
        if slot == 3:
            for half in range(2):
                token_on(half).wait_recv()
        else:
            token_copy(slot == 1, 2 - slot).wait_recv()
        id_copy(slot).wait_recv()
        key[slot] = keys(slot)

    def arrive_t(e, slot):
        exchanged(*out_t(e, slot)).wait_recv()
        unpack(came_t.at[e, slot], rows.at[e], slot * ROWS, 0)

    def arrive_s(e):
        exchanged(*out_s(e)).wait_recv()
        unpack(came_s.at[e], rows.at[e], 0, WIDTH)

    def gather_copy(e, from_slot, to_slot, half, n, to):
        a, b = from_slot * ROWS + half * HALF, to_slot * ROWS + half * HALF
        return remote(
            rows.at[e, a : a + HALF, WIDTH:D], rows.at[e, b : b + HALF, WIDTH:D],
            z_send.at[e, n], z_recv.at[e, to_slot, half], (to, m),
        )

    def gather_up(e, half):
        return gather_copy(e, 0, 1, half, half, above)

    def gather_down(e, half):
        return gather_copy(e, 0, 2, half, 2 + half, below)

    def gather_on(e, half):
        return gather_copy(e, 1 + half, 3, half, 4 + half, (above, below)[half])

    def gather(e):
        for half in range(2):
            gather_up(e, half).start()
            gather_down(e, 1 - half).start()

    def pass_on(e):
        gather_up(e, 0).wait_recv()
        gather_on(e, 0).start()
        gather_down(e, 1).wait_recv()
        gather_on(e, 1).start()

    def gathered(e):
        gather_up(e, 1).wait_recv()
        gather_down(e, 0).wait_recv()
        for half in range(2):
            gather_on(e, half).wait_recv()

    def ring(block, relay, home, send_sem, relay_sem, home_sem):
        def copy(which):
            if which < 2:
                half = which
                return remote(
                    block(3, half), relay(half), send_sem.at[which], relay_sem.at[half],
                    ((below, above)[half], m),
                )
            k, half = ((0, 1), (1, 0), (0, 0), (1, 1))[which - 2]
            return remote(
                block(1 + k, half), home(k, half), send_sem.at[which], home_sem.at[k, half],
                ((below, above)[k], m),
            )

        def start(*which):
            for n in which:
                copy(n).start()

        def pass_sum():
            for k in range(2):
                copy(k).wait_recv()
                mine, arrived = block(1 + k, k), relay(k)

                @pl.loop(0, 4)
                def _(j):
                    cols = pl.ds(pl.multiple_of(j * 512, 512), 512)
                    mine[:, cols] = (
                        mine[:, cols].astype(F32) + arrived[:, cols].astype(F32)
                    ).astype(BF16)

                copy(4 + k).start()

        def wait_home():
            for which in range(2, 6):
                copy(which).wait_recv()

        def wait_sent():
            for which in range(6):
                copy(which).wait_send()

        return start, pass_sum, wait_home, wait_sent

    def ring_s(e, s):
        def block(slot, half):
            return part_s.at[e, s, slot * ROWS + half * HALF : slot * ROWS + (half + 1) * HALF]

        return ring(
            block,
            lambda half: relay_s.at[e, s, half * HALF : (half + 1) * HALF],
            lambda k, half: home_s.at[e, s, k, half * HALF : (half + 1) * HALF],
            ps_send.at[e, s], rs_recv.at[e, s], hs_recv.at[e, s],
        )

    def block_t(s, slot, lo, hi):
        top, left = slot // 2 * 128, slot % 2 * WIDTH
        return down.at[s, top + lo : top + hi, left : left + WIDTH]

    def ring_t(s):
        return ring(
            lambda slot, half: block_t(s, slot, half * 64, half * 64 + 64),
            lambda half: relay_t.at[s, half * 64 : half * 64 + 64],
            lambda k, half: home_t.at[s, k, half * 64 : half * 64 + 64],
            pt_send.at[s], rt_recv.at[s], ht_recv.at[s],
        )

    def multiply(e, s):
        @pl.loop(0, 3)
        def _(k):
            cols = pl.ds(pl.multiple_of(k * 256, 256), 256)
            acc[:, cols] = jnp.dot(rows[e, :, :], wide[s, :, cols], preferred_element_type=F32)

        @pl.loop(0, 8)
        def _(i):
            at = pl.ds(pl.multiple_of(i * HALF, HALF), HALF)
            gate = acc[at, 0:Q]
            hidden[at, :] = (gate / (1.0 + jnp.exp(-gate)) * acc[at, Q : 2 * Q]).astype(BF16)

        def project(target, left):
            @pl.loop(0, 4)
            def _(j):
                cols = pl.ds(pl.multiple_of(j * 512, 512), 512)
                from_cols = pl.ds(pl.multiple_of(left + j * 512, 512), 512)
                target[:, cols] = jnp.dot(
                    hidden[...], down[s, :, from_cols], preferred_element_type=F32
                ).astype(BF16)

        project(part_s.at[e, s], WIDTH)
        ring_s(e, s)[0](0, 1, 2, 3)
        project(part_t, 0)
        for slot in (3, 1, 2, 0):
            pack(part_t, slot * ROWS, in_t(e, s, slot)[0])
            exchange(*in_t(e, s, slot), 1)

    def finish_s(e, s):
        ring_s(e, s)[2]()

        @pl.loop(0, 4)
        def _(j):
            cols = pl.ds(pl.multiple_of(j * 512, 512), 512)
            part_s[e, s, 0:ROWS, cols] = (
                part_s[e, s, 0:ROWS, cols].astype(F32)
                + home_s[e, s, 0, :, cols].astype(F32)
                + home_s[e, s, 1, :, cols].astype(F32)
            ).astype(BF16)

        pack(part_s.at[e, s], 0, in_s(e, s)[0])
        exchange(*in_s(e, s), 1)

    def collect_t(s):
        for slot in (3, 1, 2, 0):
            for e in range(2):
                exchanged(*in_t(e, s, slot)).wait_recv()
                unpack(in_t(e, s, slot)[1], rows.at[1], slot * ROWS, e * WIDTH)
            first, second = to_tokens(key[slot][0], 0), to_tokens(key[slot][0], 1)
            at = slice(slot * ROWS, (slot + 1) * ROWS)
            for j in range(2):
                cols = slice(j * 1024, (j + 1) * 1024)
                cols_1 = slice(WIDTH + j * 1024, WIDTH + (j + 1) * 1024)
                block_t(s, slot, 0, 128)[:, cols] = (
                    jnp.dot(first, rows[1, at, cols], preferred_element_type=F32)
                    + jnp.dot(second, rows[1, at, cols_1], preferred_element_type=F32)
                ).astype(BF16)
            ring_t(s)[0](*{3: (0, 1), 1: (2,), 2: (3,), 0: ()}[slot])

    def result_copy(s, n):
        source = (down.at[s, 0:128, 0:WIDTH], down.at[s, 256:384, WIDTH:D])[n]
        target = (out_plus, out_minus)[s].at[:, n * WIDTH : (n + 1) * WIDTH]
        return pltpu.make_async_copy(source, target, o_sem.at[s, n])

    def result_s(s):
        for e in range(2):
            exchanged(*in_s(e, s)).wait_recv()
            unpack(in_s(e, s)[1], rows.at[0], 0, e * WIDTH)
        first, second = to_tokens(key[0][0], 0), to_tokens(key[0][0], 1)

        @pl.loop(0, 2)
        def _(j):
            cols = pl.ds(pl.multiple_of(j * 1024, 1024), 1024)
            cols_1 = pl.ds(pl.multiple_of(WIDTH + j * 1024, 1024), 1024)
            picked = jnp.dot(
                first, rows[0, 0:ROWS, cols], preferred_element_type=F32
            ) + jnp.dot(second, rows[0, 0:ROWS, cols_1], preferred_element_type=F32)
            down[s, 256:384, cols_1] = picked.astype(BF16)

        result_copy(s, 1).start()

    def result_t(s):
        ring_t(s)[2]()

        @pl.loop(0, 4)
        def _(j):
            cols = pl.ds(pl.multiple_of(j * 512, 512), 512)
            down[s, 0:128, cols] = (
                down[s, 0:128, cols].astype(F32)
                + home_t[s, 0, :, cols].astype(F32)
                + home_t[s, 1, :, cols].astype(F32)
            ).astype(BF16)

        result_copy(s, 0).start()

    dispatch_t(0, 0)
    dispatch_s(0)
    dispatch_t(1, 0)
    loads[0].wait()
    loads[1].wait()
    move_wide(0, 0, 24)
    tokens_on()
    move_wide(0, 24, 56)
    for slot in (1, 2):
        tokens_there(slot)
        dispatch_t(0, slot)
    arrive_s(0)
    gather(0)
    move_wide(0, 56, 88)
    tokens_there(3)
    dispatch_t(0, 3)
    dispatch_s(1)
    for slot in (1, 2, 3):
        dispatch_t(1, slot)
    move_wide(0, 88, 128)
    pass_on(0)
    loads[2].wait()
    move_down(0, 0, 48)
    arrive_t(0, 0)
    arrive_s(1)
    gather(1)
    move_down(0, 48, 96)
    for slot in (1, 2, 3):
        arrive_t(0, slot)
    gathered(0)
    multiply(0, 0)
    pass_on(1)
    multiply(0, 1)
    loads = load_weights(1)
    for copy in loads:
        copy.start()
    for slot in range(4):
        arrive_t(1, slot)

    @pl.loop(1, PEERS)
    def _(p):
        pl.semaphore_signal(free_sem, inc=1, device_id=(z, peer(p, -1)), device_id_type=MESH)

    loads[0].wait()
    loads[1].wait()
    move_wide(1, 0, 32)
    ring_s(0, 0)[1]()
    move_wide(1, 32, 96)
    ring_s(0, 1)[1]()
    move_wide(1, 96, 128)
    loads[2].wait()
    move_down(1, 0, 96)
    gathered(1)
    for e in range(2):
        for slot in range(4):
            exchanged(*out_t(e, slot)).wait_send()
        exchanged(*out_s(e)).wait_send()
        for half in range(2):
            for copy in (gather_up(e, half), gather_down(e, half), gather_on(e, half)):
                copy.wait_send()
    pl.semaphore_wait(free_sem, PEERS - 1)
    multiply(1, 0)
    multiply(1, 1)
    finish_s(0, 0)
    ring_s(1, 0)[1]()
    finish_s(0, 1)
    ring_s(1, 1)[1]()
    collect_t(0)
    finish_s(1, 0)
    ring_t(0)[1]()
    finish_s(1, 1)
    collect_t(1)
    result_s(0)
    ring_t(1)[1]()
    result_t(0)
    result_s(1)
    result_t(1)

    for slot in (1, 2, 3):
        id_copy(slot).wait_send()
    for half in range(2):
        token_copy(True, half).wait_send()
        token_copy(False, half).wait_send()
        token_on(half).wait_send()
    for e in range(2):
        for s in range(2):
            ring_s(e, s)[3]()
            exchanged(*in_s(e, s)).wait_send()
            for slot in range(4):
                exchanged(*in_t(e, s, slot)).wait_send()
    for s in range(2):
        ring_t(s)[3]()
        for n in range(2):
            result_copy(s, n).wait()


def shards(tokens, expert_ids, gate_probs, gate_weight, up_weight, down_weight, sign_offset):
    at = np.arange(256)
    swap = (at % 16 * 16 + at // 16).astype(np.int32).reshape(256, 1)
    slot = np.arange(ROWS)
    peer = slot % PEERS
    slots = np.stack([peer // 8, peer // 2 % 4, peer % 2, slot // PEERS], axis=1).astype(np.int32)
    vmem, hbm = pl.BlockSpec(memory_space=pltpu.VMEM), pl.BlockSpec(memory_space=pl.ANY)
    smem = pl.BlockSpec(memory_space=pltpu.SMEM)
    dma = pltpu.SemaphoreType.DMA
    plus, minus = pl.pallas_call(
        kernel,
        out_shape=[jax.ShapeDtypeStruct((128, D), BF16)] * 2,
        in_specs=[vmem, smem, vmem, vmem, vmem, vmem, hbm, hbm, hbm],
        out_specs=[hbm, hbm],
        scratch_shapes=[
            pltpu.VMEM((4, 8, 128), I32),
            pltpu.VMEM((3, 128, WIDTH), BF16),
            pltpu.VMEM((2, 4 * ROWS, D), BF16),
            pltpu.VMEM((4, 4, PEERS * MSG, 128), BF16),
            pltpu.VMEM((2, 4, PEERS * MSG, 128), BF16),
            pltpu.VMEM((2, 4, PEERS * MSG, 128), BF16),
            pltpu.VMEM((4, PEERS * MSG, 128), BF16),
            pltpu.VMEM((2, PEERS * MSG, 128), BF16),
            pltpu.VMEM((2, PEERS * MSG, 128), BF16),
            pltpu.VMEM((2, D, 2 * Q), BF16),
            pltpu.VMEM((2, Q, D), BF16),
            pltpu.VMEM((4 * ROWS, WIDTH), BF16),
            pltpu.VMEM((2, 2, 4 * ROWS, WIDTH), BF16),
            pltpu.VMEM((2, 2, ROWS, WIDTH), BF16),
            pltpu.VMEM((2, 2, 2, ROWS, WIDTH), BF16),
            pltpu.VMEM((2, 128, WIDTH), BF16),
            pltpu.VMEM((2, 2, 128, WIDTH), BF16),
            pltpu.VMEM((4 * ROWS, 2 * Q), F32),
            pltpu.VMEM((4 * ROWS, Q), BF16),
            pltpu.VMEM((256, 256), BF16),
            dma((3,)),
            dma((3,)),
            dma((3,)),
            dma((3, 2)),
            dma((3, 2)),
            dma((2,)),
            dma((2,)),
            dma((2, 4)),
            dma((2, 4)),
            dma((2, 6)),
            dma((2, 4, 2)),
            dma((2, 2, 6)),
            dma((2, 2, 2)),
            dma((2, 2, 2, 2)),
            dma((2, 6)),
            dma((2, 2)),
            dma((2, 2, 2)),
            dma((4,)),
            dma((4,)),
            dma((4, 4)),
            dma((4, 4)),
            dma((2, 2)),
            pltpu.SemaphoreType.REGULAR,
        ],
        compiler_params=pltpu.CompilerParams(
            collective_id=0, has_side_effects=True, vmem_limit_bytes=65_500_000
        ),
    )(
        expert_ids.reshape(1, 128),
        sign_offset,
        jnp.asarray(swap),
        jnp.asarray(slots),
        jnp.asarray(slots.T),
        tokens,
        gate_weight,
        up_weight,
        down_weight,
    )
    return pl.pallas_call(
        weigh,
        out_shape=[jax.ShapeDtypeStruct((128, D), BF16)] * 2,
        in_specs=[vmem] * 3,
        out_specs=[vmem] * 2,
    )(gate_probs.reshape(1, 128), plus, minus)


def solution(mesh):
    in_specs = (
        P(("dp", "mp"), None),
        P(("dp", "mp"), None),
        P(("dp", "mp"), None),
        P("mp", None, "dp"),
        P("mp", None, "dp"),
        P("mp", "dp", None),
        P(),
    )
    out_specs = (P(("dp", "mp"), None), P(("dp", "mp"), None))
    return jax.shard_map(shards, mesh=mesh, in_specs=in_specs, out_specs=out_specs, check_vma=False)
```

```python
import jax
import jax.numpy as jnp
import numpy as np
from jax import lax
from jax.experimental import pallas as pl
from jax.experimental.pallas import tpu as pltpu
from jax.sharding import PartitionSpec as P

D = 4096
FF = 1536
Q = 384
CAP = 3
ROWS = 96
HALF = 48
WIDTH = 2048
MSG = 48
PEERS = 32
EPS = 0.005
MESH = pl.DeviceIdType.MESH
F32, BF16, I32 = jnp.float32, jnp.bfloat16, jnp.int32


def mixing(number):
    number = number ^ lax.shift_right_logical(number, jnp.full_like(number, 16))
    number = number * 73244475
    number = number ^ lax.shift_right_logical(number, jnp.full_like(number, 16))
    number = number * 73244475
    return number ^ lax.shift_right_logical(number, jnp.full_like(number, 16))


def moved_by(position, offset_mixed):
    hashed = mixing(position ^ offset_mixed)
    return jnp.where((hashed & 512) != 0, EPS, -EPS).astype(F32)


def weigh(probs_row, plus, minus, out_plus, out_minus):
    same = lax.broadcasted_iota(I32, (128, 128), 0) == lax.broadcasted_iota(I32, (128, 128), 1)
    probs = jnp.sum(jnp.where(same, probs_row[...], 0.0), axis=1, keepdims=True)
    out_plus[...] = (probs * plus[...].astype(F32)).astype(BF16)
    out_minus[...] = (probs * minus[...].astype(F32)).astype(BF16)


def kernel(
    ids_row, sign_offset, swap, slots_col, slots_row, tokens, gate_w, up_w, down_w,
    out_plus, out_minus,
    ids_all, others, rows, sent_t, came_t, back_t, sent_s, came_s, back_s, wide, down, part_t, part_s,
    relay_s, home_s, relay_t, home_t, acc, hidden, perm,
    w_sem, i_send, i_recv, t_send, t_recv, xs_send, xs_recv, xt_send, xt_recv, z_send, z_recv,
    ps_send, rs_recv, hs_recv, pt_send, rt_recv, ht_recv, bs_send, bs_recv, bt_send, bt_recv, o_sem,
    free_sem,
):
    z, m = lax.axis_index("dp"), lax.axis_index("mp")
    x, y, core = lax.div(m, 8), lax.rem(lax.div(m, 2), 4), lax.rem(m, 2)
    above, below, across = (z + 1) % 4, (z + 3) % 4, (z + 2) % 4
    hidden_base = z * Q

    def peer(p, sign):
        a, b = lax.div(p, 8), lax.rem(lax.div(p, 2), 4)
        return (
            lax.rem(x + sign * a + 4, 4) * 8
            + lax.rem(y + sign * b + 4, 4) * 2
            + lax.rem(core + p, 2)
        )

    def remote(source, target, send_sem, recv_sem, device):
        return pltpu.make_async_remote_copy(
            source, target, send_sem, recv_sem, device_id=device, device_id_type=MESH
        )

    def load_weights(e):
        return [
            pltpu.make_async_copy(source.at[e], target, w_sem.at[i])
            for i, (source, target) in enumerate(
                (
                    (gate_w, wide.at[0, :, 0:Q]),
                    (up_w, wide.at[0, :, Q : 2 * Q]),
                    (down_w, down.at[0]),
                )
            )
        ]

    loads = load_weights(0)
    for copy in loads:
        copy.start()

    barrier = pltpu.get_barrier_semaphore()

    @pl.loop(1, PEERS)
    def _(p):
        pl.semaphore_signal(barrier, inc=1, device_id=(z, peer(p, -1)), device_id_type=MESH)

    for near in (above, below, across):
        pl.semaphore_signal(barrier, inc=1, device_id=(near, m), device_id_type=MESH)
    ids_all[0] = jnp.broadcast_to(ids_row[...], (8, 128))
    pl.semaphore_wait(barrier, PEERS + 2)

    def token_copy(up, half):
        at = slice(half * 64, half * 64 + 64)
        return remote(
            tokens.at[at, 0:WIDTH], others.at[0 if up else 1, at], t_send.at[0 if up else 1, half],
            t_recv.at[0 if up else 1, half], (above if up else below, m),
        )

    def token_on(half):
        at = slice(half * 64, half * 64 + 64)
        return remote(
            others.at[half, at], others.at[2, at], t_send.at[2, half], t_recv.at[2, half],
            ((above, below)[half], m),
        )

    def id_copy(slot):
        device = (above, below, across)[slot - 1]
        return remote(
            ids_all.at[0], ids_all.at[slot], i_send.at[slot - 1], i_recv.at[slot - 1], (device, m)
        )

    for slot in (1, 2, 3):
        id_copy(slot).start()
    for half in range(2):
        token_copy(True, half).start()
        token_copy(False, 1 - half).start()

    at_row = lax.broadcasted_iota(I32, (128, 128), 0)
    at_col = lax.broadcasted_iota(I32, (128, 128), 1)

    def as_column(row):
        return jnp.sum(jnp.where(at_row == at_col, row, jnp.zeros_like(row)), axis=1, keepdims=True)

    def keys(slot):
        row = ids_all[slot][0:1]
        column = as_column(row)
        alike = column == row
        key_col = column * 4 + jnp.sum(
            jnp.where(alike & (at_col < at_row), 1, 0), axis=1, keepdims=True
        )
        key_row = row * 4 + jnp.sum(
            jnp.where(alike & (at_row < at_col), 1, 0), axis=0, keepdims=True
        )
        return key_col, key_row

    def slot_keys(a, b, d, s, e):
        owner = ((x - a) & 3) * 8 + ((y - b) & 3) * 2 + ((core + d) & 1)
        return (owner * 2 + e) * 4 + s

    def one_hot(found):
        return jnp.where(found, 1.0, 0.0).astype(BF16)

    def to_slots(key_row, e):
        return one_hot(key_row == slot_keys(*[slots_col[:, i : i + 1] for i in range(4)], e))

    def to_tokens(key_col, e):
        return one_hot(key_col == slot_keys(*[slots_row[i : i + 1, :] for i in range(4)], e))

    perm[...] = one_hot(lax.broadcasted_iota(I32, (256, 256), 1) == swap[...])

    def swapped(value):
        return jnp.dot(perm[...], value, preferred_element_type=F32).astype(BF16)

    def pack(source, first, target):
        laid = swapped(
            jnp.concatenate(
                [
                    jnp.concatenate(
                        [
                            source[first + k * 16 : first + (k + 1) * 16, c * 128 : (c + 1) * 128]
                            for k in range(2 * CAP)
                        ],
                        axis=1,
                    )
                    for c in range(16)
                ],
                axis=0,
            )
        )
        for k in range(2 * CAP):
            for p in range(16):
                to = (k % 2 * 16 + p) * MSG + k // 2 * 16
                target[to : to + 16, :] = laid[p * 16 : (p + 1) * 16, k * 128 : (k + 1) * 128]

    def unpack(source, target, first, left):
        laid = swapped(
            jnp.concatenate(
                [
                    jnp.concatenate(
                        [
                            source[
                                (k % 2 * 16 + p) * MSG + k // 2 * 16 : (k % 2 * 16 + p) * MSG
                                + (k // 2 + 1) * 16,
                                :,
                            ]
                            for k in range(2 * CAP)
                        ],
                        axis=1,
                    )
                    for p in range(16)
                ],
                axis=0,
            )
        )
        for k in range(2 * CAP):
            for c in range(16):
                target[
                    first + k * 16 : first + (k + 1) * 16, left + c * 128 : left + (c + 1) * 128
                ] = laid[c * 16 : (c + 1) * 16, k * 128 : (k + 1) * 128]

    def exchange(source, target, send_sem, recv_sem, sign):
        @pl.loop(1, PEERS)
        def _(p):
            at = pl.ds(pl.multiple_of(p * MSG, MSG), MSG)
            remote(
                source.at[at], target.at[at], send_sem, recv_sem, (z, peer(p, sign))
            ).start()

        target[0:MSG, :] = source[0:MSG, :]

    def exchanged(source, target, send_sem, recv_sem):
        return remote(
            source.at[MSG : PEERS * MSG], target.at[MSG : PEERS * MSG], send_sem, recv_sem,
            (z, peer(jnp.int32(1), 1)),
        )

    def out_s(e):
        return sent_s.at[e], came_s.at[e], xs_send.at[e], xs_recv.at[e]

    def out_t(e, slot):
        return sent_t.at[e, slot], came_t.at[e, slot], xt_send.at[e, slot], xt_recv.at[e, slot]

    def in_s(e, s):
        i = 2 * e + s
        if e == 0:
            return sent_s.at[2 + s], back_s.at[s], bs_send.at[i], bs_recv.at[i]
        return sent_s.at[s], came_s.at[s], bs_send.at[i], bs_recv.at[i]

    def in_t(e, s, slot):
        i = 2 * e + s
        if e == 0:
            return sent_t.at[2 + s, slot], back_t.at[s, slot], bt_send.at[i, slot], bt_recv.at[i, slot]
        return sent_t.at[s, slot], came_t.at[s, slot], bt_send.at[i, slot], bt_recv.at[i, slot]

    key = {0: keys(0)}

    def select(e, slot, value, target, first):
        chosen = to_slots(key[slot][1], e)
        for c in range(2):
            target[first : first + ROWS, c * 1024 : (c + 1) * 1024] = jnp.dot(
                chosen, value(slice(c * 1024, (c + 1) * 1024)), preferred_element_type=F32
            ).astype(BF16)

    def dispatch_s(e):
        staged = part_s.at[0, e]
        select(e, 0, lambda cols: tokens[:, WIDTH + cols.start : WIDTH + cols.stop], staged, 0)
        pack(staged, 0, sent_s.at[e])
        exchange(*out_s(e), -1)

    def dispatch_t(e, slot):
        value = (lambda cols: tokens[:, cols]) if slot == 0 else (lambda cols: others[slot - 1, :, cols])
        select(e, slot, value, part_t, slot * ROWS)
        pack(part_t, slot * ROWS, sent_t.at[e, slot])
        exchange(*out_t(e, slot), -1)

    offset_mixed = mixing(sign_offset[0] * 668265261 + 12345)

    def move_wide(e, lo, hi):
        expert = m * 2 + e
        inner = lax.broadcasted_iota(I32, (32, Q), 0) * (3 * FF) + lax.broadcasted_iota(
            I32, (32, Q), 1
        ) * 3

        @pl.loop(lo, hi)
        def _(i):
            at = pl.ds(pl.multiple_of(i * 32, 32), 32)
            first = ((expert * D + i * 32) * FF + hidden_base) * 3
            for tag in range(2):
                cols = slice(tag * Q, (tag + 1) * Q)
                weight = wide[0, at, cols].astype(F32)
                step = moved_by(inner + (first + tag), offset_mixed)
                wide[0, at, cols] = (weight + step).astype(BF16)
                wide[1, at, cols] = (weight - step).astype(BF16)

    def move_down(e, lo, hi):
        expert = m * 2 + e
        inner = lax.broadcasted_iota(I32, (32, 512), 0) * (3 * D) + lax.broadcasted_iota(
            I32, (32, 512), 1
        ) * 3

        @pl.loop(lo, hi)
        def _(i):
            row, col = i // 8 * 32, i % 8 * 512
            at, cols = pl.ds(pl.multiple_of(row, 32), 32), pl.ds(pl.multiple_of(col, 512), 512)
            first = ((expert * FF + hidden_base + row) * D + col) * 3 + 2
            weight = down[0, at, cols].astype(F32)
            step = moved_by(inner + first, offset_mixed)
            down[0, at, cols] = (weight + step).astype(BF16)
            down[1, at, cols] = (weight - step).astype(BF16)

    def tokens_on():
        token_copy(True, 0).wait_recv()
        token_on(0).start()
        token_copy(False, 1).wait_recv()
        token_on(1).start()

    def tokens_there(slot):
        if slot == 3:
            for half in range(2):
                token_on(half).wait_recv()
        else:
            token_copy(slot == 1, 2 - slot).wait_recv()
        id_copy(slot).wait_recv()
        key[slot] = keys(slot)

    def arrive_t(e, slot):
        exchanged(*out_t(e, slot)).wait_recv()
        unpack(came_t.at[e, slot], rows.at[e], slot * ROWS, 0)

    def arrive_s(e):
        exchanged(*out_s(e)).wait_recv()
        unpack(came_s.at[e], rows.at[e], 0, WIDTH)

    def gather_copy(e, from_slot, to_slot, half, n, to):
        a, b = from_slot * ROWS + half * HALF, to_slot * ROWS + half * HALF
        return remote(
            rows.at[e, a : a + HALF, WIDTH:D], rows.at[e, b : b + HALF, WIDTH:D],
            z_send.at[e, n], z_recv.at[e, to_slot, half], (to, m),
        )

    def gather_up(e, half):
        return gather_copy(e, 0, 1, half, half, above)

    def gather_down(e, half):
        return gather_copy(e, 0, 2, half, 2 + half, below)

    def gather_on(e, half):
        return gather_copy(e, 1 + half, 3, half, 4 + half, (above, below)[half])

    def gather(e):
        for half in range(2):
            gather_up(e, half).start()
            gather_down(e, 1 - half).start()

    def pass_on(e):
        gather_up(e, 0).wait_recv()
        gather_on(e, 0).start()
        gather_down(e, 1).wait_recv()
        gather_on(e, 1).start()

    def gathered(e):
        gather_up(e, 1).wait_recv()
        gather_down(e, 0).wait_recv()
        for half in range(2):
            gather_on(e, half).wait_recv()

    def ring(block, relay, home, send_sem, relay_sem, home_sem):
        def copy(which):
            if which < 2:
                half = which
                return remote(
                    block(3, half), relay(half), send_sem.at[which], relay_sem.at[half],
                    ((below, above)[half], m),
                )
            k, half = ((0, 1), (1, 0), (0, 0), (1, 1))[which - 2]
            return remote(
                block(1 + k, half), home(k, half), send_sem.at[which], home_sem.at[k, half],
                ((below, above)[k], m),
            )

        def start(*which):
            for n in which:
                copy(n).start()

        def pass_sum():
            for k in range(2):
                copy(k).wait_recv()
                mine, arrived = block(1 + k, k), relay(k)

                @pl.loop(0, 4)
                def _(j):
                    cols = pl.ds(pl.multiple_of(j * 512, 512), 512)
                    mine[:, cols] = (
                        mine[:, cols].astype(F32) + arrived[:, cols].astype(F32)
                    ).astype(BF16)

                copy(4 + k).start()

        def wait_home():
            for which in range(2, 6):
                copy(which).wait_recv()

        def wait_sent():
            for which in range(6):
                copy(which).wait_send()

        return start, pass_sum, wait_home, wait_sent

    def ring_s(e, s):
        def block(slot, half):
            return part_s.at[e, s, slot * ROWS + half * HALF : slot * ROWS + (half + 1) * HALF]

        return ring(
            block,
            lambda half: relay_s.at[e, s, half * HALF : (half + 1) * HALF],
            lambda k, half: home_s.at[e, s, k, half * HALF : (half + 1) * HALF],
            ps_send.at[e, s], rs_recv.at[e, s], hs_recv.at[e, s],
        )

    def block_t(s, slot, lo, hi):
        top, left = slot // 2 * 128, slot % 2 * WIDTH
        return down.at[s, top + lo : top + hi, left : left + WIDTH]

    def ring_t(s):
        return ring(
            lambda slot, half: block_t(s, slot, half * 64, half * 64 + 64),
            lambda half: relay_t.at[s, half * 64 : half * 64 + 64],
            lambda k, half: home_t.at[s, k, half * 64 : half * 64 + 64],
            pt_send.at[s], rt_recv.at[s], ht_recv.at[s],
        )

    def multiply(e, s):
        @pl.loop(0, 3)
        def _(k):
            cols = pl.ds(pl.multiple_of(k * 256, 256), 256)
            acc[:, cols] = jnp.dot(rows[e, :, :], wide[s, :, cols], preferred_element_type=F32)

        @pl.loop(0, 8)
        def _(i):
            at = pl.ds(pl.multiple_of(i * HALF, HALF), HALF)
            gate = acc[at, 0:Q]
            hidden[at, :] = (gate / (1.0 + jnp.exp(-gate)) * acc[at, Q : 2 * Q]).astype(BF16)

        def project(target, left):
            @pl.loop(0, 4)
            def _(j):
                cols = pl.ds(pl.multiple_of(j * 512, 512), 512)
                from_cols = pl.ds(pl.multiple_of(left + j * 512, 512), 512)
                target[:, cols] = jnp.dot(
                    hidden[...], down[s, :, from_cols], preferred_element_type=F32
                ).astype(BF16)

        project(part_s.at[e, s], WIDTH)
        ring_s(e, s)[0](0, 1, 2, 3)
        project(part_t, 0)
        for slot in (3, 1, 2, 0):
            pack(part_t, slot * ROWS, in_t(e, s, slot)[0])
            exchange(*in_t(e, s, slot), 1)

    def finish_s(e, s):
        ring_s(e, s)[2]()

        @pl.loop(0, 4)
        def _(j):
            cols = pl.ds(pl.multiple_of(j * 512, 512), 512)
            part_s[e, s, 0:ROWS, cols] = (
                part_s[e, s, 0:ROWS, cols].astype(F32)
                + home_s[e, s, 0, :, cols].astype(F32)
                + home_s[e, s, 1, :, cols].astype(F32)
            ).astype(BF16)

        pack(part_s.at[e, s], 0, in_s(e, s)[0])
        exchange(*in_s(e, s), 1)

    def collect_t(s):
        for slot in (3, 1, 2, 0):
            for e in range(2):
                exchanged(*in_t(e, s, slot)).wait_recv()
                unpack(in_t(e, s, slot)[1], rows.at[1], slot * ROWS, e * WIDTH)
            first, second = to_tokens(key[slot][0], 0), to_tokens(key[slot][0], 1)
            at = slice(slot * ROWS, (slot + 1) * ROWS)
            for j in range(2):
                cols = slice(j * 1024, (j + 1) * 1024)
                cols_1 = slice(WIDTH + j * 1024, WIDTH + (j + 1) * 1024)
                block_t(s, slot, 0, 128)[:, cols] = (
                    jnp.dot(first, rows[1, at, cols], preferred_element_type=F32)
                    + jnp.dot(second, rows[1, at, cols_1], preferred_element_type=F32)
                ).astype(BF16)
            ring_t(s)[0](*{3: (0, 1), 1: (2,), 2: (3,), 0: ()}[slot])

    def result_copy(s, n):
        source = (down.at[s, 0:128, 0:WIDTH], down.at[s, 256:384, WIDTH:D])[n]
        target = (out_plus, out_minus)[s].at[:, n * WIDTH : (n + 1) * WIDTH]
        return pltpu.make_async_copy(source, target, o_sem.at[s, n])

    def result_s(s):
        for e in range(2):
            exchanged(*in_s(e, s)).wait_recv()
            unpack(in_s(e, s)[1], rows.at[0], 0, e * WIDTH)
        first, second = to_tokens(key[0][0], 0), to_tokens(key[0][0], 1)

        @pl.loop(0, 2)
        def _(j):
            cols = pl.ds(pl.multiple_of(j * 1024, 1024), 1024)
            cols_1 = pl.ds(pl.multiple_of(WIDTH + j * 1024, 1024), 1024)
            picked = jnp.dot(
                first, rows[0, 0:ROWS, cols], preferred_element_type=F32
            ) + jnp.dot(second, rows[0, 0:ROWS, cols_1], preferred_element_type=F32)
            down[s, 256:384, cols_1] = picked.astype(BF16)

        result_copy(s, 1).start()

    def result_t(s):
        ring_t(s)[2]()

        @pl.loop(0, 4)
        def _(j):
            cols = pl.ds(pl.multiple_of(j * 512, 512), 512)
            down[s, 0:128, cols] = (
                down[s, 0:128, cols].astype(F32)
                + home_t[s, 0, :, cols].astype(F32)
                + home_t[s, 1, :, cols].astype(F32)
            ).astype(BF16)

        result_copy(s, 0).start()

    dispatch_t(0, 0)
    dispatch_s(0)
    dispatch_s(1)
    dispatch_t(1, 0)
    loads[0].wait()
    loads[1].wait()
    move_wide(0, 0, 24)
    tokens_on()
    move_wide(0, 24, 56)
    for slot in (1, 2):
        tokens_there(slot)
        dispatch_t(0, slot)
    arrive_s(0)
    gather(0)
    move_wide(0, 56, 88)
    tokens_there(3)
    dispatch_t(0, 3)
    for slot in (1, 2, 3):
        dispatch_t(1, slot)
    move_wide(0, 88, 128)
    pass_on(0)
    arrive_s(1)
    gather(1)
    loads[2].wait()
    move_down(0, 0, 48)
    arrive_t(0, 0)
    move_down(0, 48, 96)
    for slot in (1, 2, 3):
        arrive_t(0, slot)
    gathered(0)
    multiply(0, 0)
    pass_on(1)
    multiply(0, 1)
    loads = load_weights(1)
    for copy in loads:
        copy.start()
    for slot in range(4):
        arrive_t(1, slot)

    @pl.loop(1, PEERS)
    def _(p):
        pl.semaphore_signal(free_sem, inc=1, device_id=(z, peer(p, -1)), device_id_type=MESH)

    loads[0].wait()
    loads[1].wait()
    move_wide(1, 0, 32)
    ring_s(0, 0)[1]()
    move_wide(1, 32, 96)
    ring_s(0, 1)[1]()
    move_wide(1, 96, 128)
    loads[2].wait()
    move_down(1, 0, 96)
    gathered(1)
    for e in range(2):
        for slot in range(4):
            exchanged(*out_t(e, slot)).wait_send()
        exchanged(*out_s(e)).wait_send()
        for half in range(2):
            for copy in (gather_up(e, half), gather_down(e, half), gather_on(e, half)):
                copy.wait_send()
    pl.semaphore_wait(free_sem, PEERS - 1)
    multiply(1, 0)
    multiply(1, 1)
    finish_s(0, 0)
    ring_s(1, 0)[1]()
    finish_s(0, 1)
    ring_s(1, 1)[1]()
    collect_t(0)
    finish_s(1, 0)
    ring_t(0)[1]()
    finish_s(1, 1)
    collect_t(1)
    result_s(0)
    ring_t(1)[1]()
    result_t(0)
    result_s(1)
    result_t(1)

    for slot in (1, 2, 3):
        id_copy(slot).wait_send()
    for half in range(2):
        token_copy(True, half).wait_send()
        token_copy(False, half).wait_send()
        token_on(half).wait_send()
    for e in range(2):
        for s in range(2):
            ring_s(e, s)[3]()
            exchanged(*in_s(e, s)).wait_send()
            for slot in range(4):
                exchanged(*in_t(e, s, slot)).wait_send()
    for s in range(2):
        ring_t(s)[3]()
        for n in range(2):
            result_copy(s, n).wait()


def shards(tokens, expert_ids, gate_probs, gate_weight, up_weight, down_weight, sign_offset):
    at = np.arange(256)
    swap = (at % 16 * 16 + at // 16).astype(np.int32).reshape(256, 1)
    slot = np.arange(ROWS)
    peer = slot % PEERS
    slots = np.stack([peer // 8, peer // 2 % 4, peer % 2, slot // PEERS], axis=1).astype(np.int32)
    vmem, hbm = pl.BlockSpec(memory_space=pltpu.VMEM), pl.BlockSpec(memory_space=pl.ANY)
    smem = pl.BlockSpec(memory_space=pltpu.SMEM)
    dma = pltpu.SemaphoreType.DMA
    plus, minus = pl.pallas_call(
        kernel,
        out_shape=[jax.ShapeDtypeStruct((128, D), BF16)] * 2,
        in_specs=[vmem, smem, vmem, vmem, vmem, vmem, hbm, hbm, hbm],
        out_specs=[hbm, hbm],
        scratch_shapes=[
            pltpu.VMEM((4, 8, 128), I32),
            pltpu.VMEM((3, 128, WIDTH), BF16),
            pltpu.VMEM((2, 4 * ROWS, D), BF16),
            pltpu.VMEM((4, 4, PEERS * MSG, 128), BF16),
            pltpu.VMEM((2, 4, PEERS * MSG, 128), BF16),
            pltpu.VMEM((2, 4, PEERS * MSG, 128), BF16),
            pltpu.VMEM((4, PEERS * MSG, 128), BF16),
            pltpu.VMEM((2, PEERS * MSG, 128), BF16),
            pltpu.VMEM((2, PEERS * MSG, 128), BF16),
            pltpu.VMEM((2, D, 2 * Q), BF16),
            pltpu.VMEM((2, Q, D), BF16),
            pltpu.VMEM((4 * ROWS, WIDTH), BF16),
            pltpu.VMEM((2, 2, 4 * ROWS, WIDTH), BF16),
            pltpu.VMEM((2, 2, ROWS, WIDTH), BF16),
            pltpu.VMEM((2, 2, 2, ROWS, WIDTH), BF16),
            pltpu.VMEM((2, 128, WIDTH), BF16),
            pltpu.VMEM((2, 2, 128, WIDTH), BF16),
            pltpu.VMEM((4 * ROWS, 2 * Q), F32),
            pltpu.VMEM((4 * ROWS, Q), BF16),
            pltpu.VMEM((256, 256), BF16),
            dma((3,)),
            dma((3,)),
            dma((3,)),
            dma((3, 2)),
            dma((3, 2)),
            dma((2,)),
            dma((2,)),
            dma((2, 4)),
            dma((2, 4)),
            dma((2, 6)),
            dma((2, 4, 2)),
            dma((2, 2, 6)),
            dma((2, 2, 2)),
            dma((2, 2, 2, 2)),
            dma((2, 6)),
            dma((2, 2)),
            dma((2, 2, 2)),
            dma((4,)),
            dma((4,)),
            dma((4, 4)),
            dma((4, 4)),
            dma((2, 2)),
            pltpu.SemaphoreType.REGULAR,
        ],
        compiler_params=pltpu.CompilerParams(
            collective_id=0, has_side_effects=True, vmem_limit_bytes=65_500_000
        ),
    )(
        expert_ids.reshape(1, 128),
        sign_offset,
        jnp.asarray(swap),
        jnp.asarray(slots),
        jnp.asarray(slots.T),
        tokens,
        gate_weight,
        up_weight,
        down_weight,
    )
    return pl.pallas_call(
        weigh,
        out_shape=[jax.ShapeDtypeStruct((128, D), BF16)] * 2,
        in_specs=[vmem] * 3,
        out_specs=[vmem] * 2,
    )(gate_probs.reshape(1, 128), plus, minus)


def solution(mesh):
    in_specs = (
        P(("dp", "mp"), None),
        P(("dp", "mp"), None),
        P(("dp", "mp"), None),
        P("mp", None, "dp"),
        P("mp", None, "dp"),
        P("mp", "dp", None),
        P(),
    )
    out_specs = (P(("dp", "mp"), None), P(("dp", "mp"), None))
    return jax.shard_map(shards, mesh=mesh, in_specs=in_specs, out_specs=out_specs, check_vma=False)
```
